32 devices in a mesh: groups: 2 (over x), seq: 16 (over z, y, core).
Axes of the slice: x: 2, y: 2, z: 4, core: 2. Of those that a mesh axis runs over, the one named last changes fastest.
Arguments:
- frames: bfloat16 [384, 256, 1280], P(('groups', 'seq')), parts along dimension 0, may hold values from -6 to 6
- match: int32 [384, 256], P(('groups', 'seq')), parts along dimension 0, may hold values from -1 to 255, as said below
- weight: int32 [384, 256], P(('groups', 'seq')), parts along dimension 0, may hold values from 1 to 8
- keep: int32 [384, 64], P(('groups', 'seq')), parts along dimension 0, may hold values from 0 to 1, as said below
- gain: float32 [1280], replicated, may hold values from 0.25 to 1.75
Outputs:
- merged_rows: bfloat16 [12288, 5120], P(('groups', 'seq')), parts along dimension 0
The draws below stay inside these ranges and needn't reach their ends.
There are 2 independent parts, one for each index of `groups`. The reference program is written for one: setup_inputs(seed, part) draws one part's arguments, and reference() takes and returns one part's arrays. A program takes and returns all parts, laid end to end along the dimension named above; an argument that names none is the same for every part. Nothing has to cross between parts.
Inputs may be any that keep to these rules, and one draw needn't show every extreme that they name: `keep`: exactly 6144 groups are kept. Frame 0 keeps all its groups and every frame keeps one or more. For each i the kept groups of frames 0 to 12 * i - 1 number 384 * i plus or minus at most 180, and exactly 180 away for some i. match[f, t] is -1 where group t // 4 of frame f is kept, and otherwise names a token of frame f - 1 whose group is kept there.
All inputs are finite; a program needn't handle non-finite values.
Results may differ from the reference program's by a relative error of at most 0.0018.
Values may be sent and summed in bfloat16 or wider, within the bound.
A program may use at most 128 MiB of HBM per device.

```python
import jax
import jax.numpy as jnp
from jax import lax

C = 1280
P_SIZE = 256
GP = 64
FR_DEV = 12
FRAMES = 192
KEPT_ROWS_LOCAL = 384
KEPT = 6144
DRIFT = 180
N_SEQ = 16


def surviving_rows(key):
    k_drift, k_spot, k_sign, force_random_key, k_rank = jax.random.split(key, 5)
    drift_walk = jax.random.randint(k_drift, (N_SEQ + 1,), -DRIFT, DRIFT + 1)
    spot = jax.random.randint(k_spot, (), 1, N_SEQ)
    polarity = jax.random.randint(k_sign, (), 0, 2) * 2 - 1
    drift_walk = drift_walk.at[spot].set(polarity * DRIFT)
    drift_walk = drift_walk.at[0].set(0).at[N_SEQ].set(0)
    kept_counts = KEPT_ROWS_LOCAL + drift_walk[1:] - drift_walk[:-1]
    chosen = jax.random.randint(force_random_key, (N_SEQ, FR_DEV), 0, GP)
    group_ids = jnp.arange(GP, dtype=jnp.int32)
    forced = group_ids[None, None, :] == chosen[:, :, None]
    opening = (jnp.arange(N_SEQ)[:, None, None] == 0) & (jnp.arange(FR_DEV)[None, :, None] == 0)
    forced = (forced | opening).reshape(N_SEQ, FR_DEV * GP).astype(jnp.int32)
    noise = jax.random.randint(k_rank, (N_SEQ, FR_DEV * GP), 0, 65536)
    score = (forced * 65536 + noise) * (FR_DEV * GP) + jnp.arange(FR_DEV * GP, dtype=jnp.int32)[None, :]
    ranking = jnp.argsort(-score, axis=1)
    position = jnp.argsort(ranking, axis=1)
    kept_tokens = (position < kept_counts[:, None]).astype(jnp.int32)
    return kept_tokens.reshape(FRAMES, GP)


def draw_keep(key, part):
    return surviving_rows(key)


def draw_match(key, part):
    kept_tokens = surviving_rows(key)
    key = jax.random.fold_in(key, 7)
    k_group, k_token = jax.random.split(key)
    prior = kept_tokens[:-1]
    totals = jnp.sum(prior, axis=1)
    picks = jax.random.randint(k_group, (FRAMES - 1, P_SIZE), 0, 1 << 20) % totals[:, None]
    running = jnp.cumsum(prior, axis=1)
    group_selection = jnp.sum((running[:, None, :] <= picks[:, :, None]).astype(jnp.int32), axis=2)
    target = group_selection * 4 + jax.random.randint(k_token, (FRAMES - 1, P_SIZE), 0, 4)
    token_group = jnp.arange(P_SIZE, dtype=jnp.int32) // 4
    dropped = kept_tokens[1:][:, token_group] == 0
    later = jnp.where(dropped, target, -1)
    return jnp.concatenate([jnp.full((1, P_SIZE), -1, jnp.int32), later.astype(jnp.int32)], axis=0)


def set_ends(entries, own_key, low, top_value):
    longest = entries.shape.index(max(entries.shape))
    spots = []
    for shift in (0, 1):
        where = [jax.random.randint(jax.random.fold_in(own_key, axis), (), 0, length) for axis, length in enumerate(entries.shape)]
        where[longest] = (where[longest] + shift) % entries.shape[longest]
        spots.append(tuple(where))
    return entries.at[spots[0]].set(low).at[spots[1]].set(top_value)


def levels(own_key, shape, cuts, least, high):
    loudness = 1.0
    for axis_at, blocks in cuts:
        heights = jax.random.uniform(jax.random.fold_in(jax.random.fold_in(own_key, 6), axis_at), (blocks,), jnp.float32, least / len(cuts), high / len(cuts))
        loudness = loudness * jnp.repeat(jnp.exp(heights), shape[axis_at] // blocks).reshape((-1,) + (1,) * (len(shape) - 1 - axis_at))
    return loudness


def normal_values(stream_key, extent, scale, bound, cuts=(), kind=jnp.bfloat16):
    drawn = scale * jax.random.normal(stream_key, extent, jnp.float32)
    if cuts:
        drawn = drawn * levels(stream_key, extent, cuts, -0.22, 0.18)
    return jnp.clip(drawn, -bound, bound).astype(kind)


def setup_inputs(seed: int = 0, part: int = 0) -> dict:
    key_list = jax.random.split(jax.random.key(seed), 6)
    part_keys = jax.random.split(jax.random.fold_in(key_list[5], part), 6)
    return {
        "frames": normal_values(part_keys[0], (FRAMES, P_SIZE, C), 1.0, 6.0, ((0, 16),)),
        "match": draw_match(jax.random.fold_in(jax.random.fold_in(key_list[5], part), 71), part),
        "weight": set_ends(jax.random.randint(part_keys[2], (FRAMES, P_SIZE), 1, 9), jax.random.fold_in(part_keys[2], 1), 1, 8).astype(jnp.int32),
        "keep": draw_keep(jax.random.fold_in(jax.random.fold_in(key_list[5], part), 71), part),
        "gain": jnp.clip(1.0 + 0.15 * jax.random.normal(key_list[4], (C,), jnp.float32), 0.25, 1.75),
    }


def reference(frames, match, weight, keep, gain):
    count_frames = frames.shape[0]
    tokens = frames.shape[1]

    def one_frame(index):
        later = jnp.minimum(index + 1, count_frames - 1)
        present = (index + 1 < count_frames).astype(jnp.float32)
        source = frames[later].astype(jnp.float32)
        targets = match[later]
        following_weight = weight[later].astype(jnp.float32) * present
        segment_ids = jnp.where(targets >= 0, targets, tokens).astype(jnp.int32)
        incoming = jax.ops.segment_sum(following_weight[:, None] * source, segment_ids, num_segments=tokens + 1)[:tokens]
        absorbed = jax.ops.segment_sum(following_weight, segment_ids, num_segments=tokens + 1)[:tokens]
        own_weight = weight[index].astype(jnp.float32)
        merged = (own_weight[:, None] * frames[index].astype(jnp.float32) + incoming) / (own_weight + absorbed)[:, None]
        scale = lax.rsqrt(lax.optimization_barrier(jnp.mean(merged * merged, axis=1, keepdims=True)) + 1e-06)
        return (merged * scale * gain).astype(jnp.bfloat16)
    normed = lax.map(one_frame, jnp.arange(count_frames, dtype=jnp.int32))
    group_rows = normed.reshape(count_frames * GP, 4 * C)
    flat_keep = keep.reshape(-1)
    kept_order = jnp.argsort(1 - flat_keep, stable=True)[:KEPT]
    return jnp.take(group_rows, kept_order, axis=0)
```

```python
import functools

import jax
import jax.numpy as jnp
from jax import lax
from jax.experimental import pallas as pl
from jax.experimental.pallas import tpu as pltpu
from jax.sharding import PartitionSpec as P

TILE = 16


def exchange_kernel(n, keep_ref, match_ref, weight_ref, all_ref, own, send_sem, recv_sem):
    me = lax.axis_index("seq")
    barrier = pltpu.get_barrier_semaphore()

    def greet(step, carry):
        peer = lax.rem(me + step, n)
        pl.semaphore_signal(
            barrier, inc=1, device_id={"seq": peer}, device_id_type=pl.DeviceIdType.MESH
        )
        return carry

    lax.fori_loop(1, n, greet, 0)
    count = jnp.sum(keep_ref[...].astype(jnp.float32), keepdims=True).astype(jnp.int32)
    own[0:1, :] = match_ref[0:1, :]
    own[1:2, :] = weight_ref[0:1, :]
    own[2:8, :] = jnp.broadcast_to(count, (6, own.shape[1]))
    all_ref[pl.ds(me, 1)] = own[...][None]
    pl.semaphore_wait(barrier, n - 1)

    def copy(step):
        peer = lax.rem(me + step, n)
        return pltpu.make_async_remote_copy(
            src_ref=own,
            dst_ref=all_ref.at[me],
            send_sem=send_sem.at[step],
            recv_sem=recv_sem.at[step],
            device_id={"seq": peer},
            device_id_type=pl.DeviceIdType.MESH,
        )

    def send(step, carry):
        copy(step).start()
        return carry

    def finish(step, carry):
        copy(step).wait()
        return carry

    lax.fori_loop(1, n, send, 0)
    lax.fori_loop(1, n, finish, 0)


def exchange(keep, match, weight):
    n = lax.axis_size("seq")
    tokens = match.shape[1]
    return pl.pallas_call(
        functools.partial(exchange_kernel, n),
        out_shape=jax.ShapeDtypeStruct((n, 8, tokens), jnp.int32),
        in_specs=[pl.BlockSpec(memory_space=pltpu.VMEM)] * 3,
        out_specs=pl.BlockSpec(memory_space=pltpu.VMEM),
        scratch_shapes=[
            pltpu.VMEM((8, tokens), jnp.int32),
            pltpu.SemaphoreType.DMA((n,)),
            pltpu.SemaphoreType.DMA((n,)),
        ],
        compiler_params=pltpu.CompilerParams(collective_id=0, has_side_effects=True),
    )(keep, match, weight)


def merge_kernel(
    side,
    starts,
    keep_ref,
    match_ref,
    weight_ref,
    next_ref,
    gain_ref,
    frame_ref,
    after_ref,
    first_ref,
    back_ref,
    own_ref,
    ahead_ref,
    window,
    own_key,
    inc_key,
    inc_weight,
    sems,
):
    count, groups = keep_ref.shape
    tokens = match_ref.shape[1]
    per = tokens // groups
    width = gain_ref.shape[1]
    rows = groups + TILE
    kept_dev = own_ref.shape[0]
    f = pl.program_id(0)

    @pl.when(f == 0)
    def _():
        keep = keep_ref[...].astype(jnp.bfloat16)
        g = lax.broadcasted_iota(jnp.int32, (groups, tokens), 0)
        t_group = lax.broadcasted_iota(jnp.int32, (groups, tokens), 1) // per
        below = (g < t_group).astype(jnp.bfloat16)
        same = (g == t_group).astype(jnp.bfloat16)
        before = jnp.dot(keep, below, preferred_element_type=jnp.float32)
        kept = jnp.dot(keep, same, preferred_element_type=jnp.float32)
        token = lax.broadcasted_iota(jnp.int32, (count, tokens), 1)
        own_key[0:count, :] = jnp.where(
            kept > 0.5, (token % per) * rows + before.astype(jnp.int32), -1000
        )
        at = lax.broadcasted_iota(jnp.int32, (groups, groups), 0)
        other = lax.broadcasted_iota(jnp.int32, (groups, groups), 1)
        column = lax.dot_general(
            (other < at).astype(jnp.bfloat16),
            keep,
            (((1,), (1,)), ((), ())),
            preferred_element_type=jnp.float32,
        )
        for k in range(count):
            if k + 1 < count:
                target = match_ref[k + 1 : k + 2, :]
                inc_weight[k : k + 1, :] = weight_ref[k + 1 : k + 2, :]
            else:
                target = next_ref[0:1, :]
                inc_weight[k : k + 1, :] = next_ref[1:2, :]
            place = jnp.sum(
                jnp.where(g == target // per, column[:, k : k + 1], 0.0), axis=0, keepdims=True
            )
            inc_key[k : k + 1, :] = jnp.where(
                target >= 0, (target % per) * rows + place.astype(jnp.int32), -1000
            )

    start = starts[f]
    base = pl.multiple_of((start // TILE) * TILE, TILE)
    off = start - base

    def work(later_ref):
        line = lax.broadcasted_iota(jnp.int32, (per * rows, tokens), 0) - off
        mine = jnp.where(
            line == own_key[pl.ds(f, 1), :], weight_ref[pl.ds(f, 1), :].astype(jnp.float32), 0.0
        )
        theirs = jnp.where(
            line == inc_key[pl.ds(f, 1), :], inc_weight[pl.ds(f, 1), :].astype(jnp.float32), 0.0
        )
        total = jnp.maximum(jnp.sum(mine + theirs, axis=1, keepdims=True), 1.0)
        summed = jnp.dot(
            mine.astype(jnp.bfloat16), frame_ref[0], preferred_element_type=jnp.float32
        ) + jnp.dot(theirs.astype(jnp.bfloat16), later_ref[0], preferred_element_type=jnp.float32)
        mean = jnp.sum(summed * summed, axis=1, keepdims=True) * (1.0 / width)
        scale = lax.rsqrt(mean + 1e-06 * total * total)
        normed = summed * scale * gain_ref[...]
        old_rows = lax.broadcasted_iota(jnp.int32, (TILE, width), 0) < off
        for j in range(per):
            cols = slice(j * width, (j + 1) * width)
            old = window[pl.ds(base, TILE), cols].astype(jnp.float32)
            head = jnp.where(old_rows, old, normed[j * rows : j * rows + TILE])
            window[pl.ds(base, TILE), cols] = head.astype(jnp.bfloat16)
            window[pl.ds(pl.multiple_of(base + TILE, TILE), groups), cols] = normed[
                j * rows + TILE : (j + 1) * rows
            ].astype(jnp.bfloat16)

    @pl.when(f < count - 1)
    def _():
        work(after_ref)

    @pl.when(f == count - 1)
    def _():
        work(first_ref)
        copies = [
            pltpu.make_async_copy(window.at[pl.ds(0, side)], back_ref, sems.at[0]),
            pltpu.make_async_copy(window.at[pl.ds(side + kept_dev, side)], ahead_ref, sems.at[1]),
            pltpu.make_async_copy(window.at[pl.ds(side, kept_dev)], own_ref, sems.at[2]),
        ]
        for copy in copies:
            copy.start()
        for copy in copies:
            copy.wait()


def merge(starts, keep, match, weight, after, gain, frames, first, side, kept_dev):
    count, tokens, width = frames.shape
    groups = keep.shape[1]
    row = tokens // groups * width
    whole = pl.BlockSpec(memory_space=pltpu.VMEM)
    return pl.pallas_call(
        functools.partial(merge_kernel, side),
        out_shape=[
            jax.ShapeDtypeStruct((side, row), jnp.bfloat16),
            jax.ShapeDtypeStruct((kept_dev, row), jnp.bfloat16),
            jax.ShapeDtypeStruct((side, row), jnp.bfloat16),
        ],
        grid_spec=pltpu.PrefetchScalarGridSpec(
            num_scalar_prefetch=1,
            grid=(count,),
            in_specs=[
                whole,
                whole,
                whole,
                whole,
                whole,
                pl.BlockSpec((1, tokens, width), lambda f, s: (f, 0, 0)),
                pl.BlockSpec((1, tokens, width), lambda f, s: (jnp.minimum(f + 1, count - 1), 0, 0)),
                pl.BlockSpec((1, tokens, width), lambda f, s: (0, 0, 0)),
            ],
            out_specs=[pl.BlockSpec(memory_space=pl.ANY)] * 3,
            scratch_shapes=[
                pltpu.VMEM((2 * side + kept_dev + groups + TILE, row), jnp.bfloat16),
                pltpu.VMEM((count, tokens), jnp.int32),
                pltpu.VMEM((count, tokens), jnp.int32),
                pltpu.VMEM((count, tokens), jnp.int32),
                pltpu.SemaphoreType.DMA((3,)),
            ],
        ),
        compiler_params=pltpu.CompilerParams(vmem_limit_bytes=48 * 1024 * 1024),
    )(starts, keep, match, weight, after, gain, frames, frames, first)


def shifted(value, steps):
    n = lax.axis_size("seq")
    pairs = [(i, i + steps) for i in range(max(0, -steps), min(n, n - steps))]
    return lax.ppermute(value, "seq", pairs)


def body(frames, match, weight, keep, gain):
    count, tokens, width = frames.shape
    groups = keep.shape[1]
    kept_dev = count * groups // 2
    drift = kept_dev // 2 - count
    side = -(-drift // TILE) * TILE
    n = lax.axis_size("seq")
    me = lax.axis_index("seq")
    first = shifted(frames[:1], -1)
    everyone = exchange(keep, match, weight)
    counts = everyone[:, 2, 0]
    device = jnp.arange(n, dtype=jnp.int32)
    drift_here = jnp.sum(jnp.where(device < me, counts - kept_dev, 0))
    drift_next = jnp.sum(jnp.where(device <= me, counts - kept_dev, 0))
    after = lax.dynamic_index_in_dim(everyone, jnp.minimum(me + 1, n - 1), 0, keepdims=False)
    after = jnp.where((me == n - 1) & (jnp.arange(8)[:, None] == 1), 0, after)
    per_frame = jnp.sum(keep, axis=1)
    frame_at = jnp.arange(count, dtype=jnp.int32)
    earlier = jnp.sum(jnp.where(frame_at[None, :] < frame_at[:, None], per_frame[None, :], 0), axis=1)
    starts = earlier + drift_here + side
    back, own, ahead = merge(
        starts, keep, match, weight, after, gain.reshape(1, width), frames, first, side, kept_dev
    )
    from_next = shifted(back, -1)
    from_before = shifted(ahead, 1)
    line = jnp.arange(side, dtype=jnp.int32)[:, None]
    top = jnp.where(line < drift_here, from_before, own[:side])
    bottom = jnp.where(line >= side + drift_next, from_next, own[kept_dev - side :])
    return jnp.concatenate([top, own[side : kept_dev - side], bottom], axis=0)


def solution(mesh):
    placed = (
        P(("groups", "seq"), None, None),
        P(("groups", "seq"), None),
        P(("groups", "seq"), None),
        P(("groups", "seq"), None),
        P(),
    )
    return jax.shard_map(
        body, mesh=mesh, in_specs=placed, out_specs=P(("groups", "seq"), None), check_vma=False
    )
```

```python
import functools

import jax
import jax.numpy as jnp
from jax import lax
from jax.experimental import pallas as pl
from jax.experimental.pallas import tpu as pltpu
from jax.sharding import PartitionSpec as P

TILE = 16


def exchange_kernel(
    n, side, chunk, keep_ref, match_ref, weight_ref, info_ref, after_ref, all_ref, own, send_sem, recv_sem
):
    count, groups = keep_ref.shape
    tokens = match_ref.shape[1]
    kept_dev = count * groups // 2
    me = lax.axis_index("seq")
    barrier = pltpu.get_barrier_semaphore()

    def greet(step, carry):
        peer = lax.rem(me + step, n)
        pl.semaphore_signal(
            barrier, inc=1, device_id={"seq": peer}, device_id_type=pl.DeviceIdType.MESH
        )
        return carry

    lax.fori_loop(1, n, greet, 0)
    keep = keep_ref[...].astype(jnp.float32)
    own[0:1, :] = match_ref[0:1, :]
    own[1:2, :] = weight_ref[0:1, :]
    total = jnp.sum(keep, keepdims=True).astype(jnp.int32)
    own[2:8, :] = jnp.broadcast_to(total, (6, tokens))
    all_ref[pl.ds(me, 1)] = own[...][None]
    pl.semaphore_wait(barrier, n - 1)

    def copy(step):
        peer = lax.rem(me + step, n)
        return pltpu.make_async_remote_copy(
            src_ref=own,
            dst_ref=all_ref.at[me],
            send_sem=send_sem.at[step],
            recv_sem=recv_sem.at[step],
            device_id={"seq": peer},
            device_id_type=pl.DeviceIdType.MESH,
        )

    def send(step, carry):
        copy(step).start()
        return carry

    def finish(step, carry):
        copy(step).wait()
        return carry

    lax.fori_loop(1, n, send, 0)
    frame = lax.broadcasted_iota(jnp.int32, keep.shape, 0)
    earlier = [
        jnp.sum(jnp.where(frame < f, keep, 0.0)).astype(jnp.int32) for f in range(count + 1)
    ]
    lax.fori_loop(1, n, finish, 0)
    counts = (all_ref[:, 2, :] - kept_dev).astype(jnp.float32)
    device = lax.broadcasted_iota(jnp.int32, counts.shape, 0)
    lane = lax.broadcasted_iota(jnp.int32, counts.shape, 1)
    counts = jnp.where(lane == 0, counts, 0.0)
    here = jnp.sum(jnp.where(device < me, counts, 0.0)).astype(jnp.int32)
    later = jnp.sum(jnp.where(device <= me, counts, 0.0)).astype(jnp.int32)
    for f in range(count + 1):
        info_ref[f] = earlier[f] + (here + side)
    odd = lax.rem(me, 2)
    outer = jnp.where(odd == 1, later, here)
    pieces = (jnp.abs(outer) + (chunk - 1)) // chunk
    info_ref[count + 1] = here
    info_ref[count + 2] = later
    info_ref[count + 3] = jnp.where(outer < 0, pieces + side // chunk, pieces)
    info_ref[count + 4] = odd
    row = lax.broadcasted_iota(jnp.int32, (8, tokens), 0)
    block = all_ref[jnp.minimum(me + 1, n - 1)]
    after_ref[...] = jnp.where((row == 1) & (me == n - 1), 0, block)


def exchange(keep, match, weight, side, chunk):
    n = lax.axis_size("seq")
    count, tokens = match.shape
    whole = pl.BlockSpec(memory_space=pltpu.VMEM)
    return pl.pallas_call(
        functools.partial(exchange_kernel, n, side, chunk),
        out_shape=[
            jax.ShapeDtypeStruct((count + 5,), jnp.int32),
            jax.ShapeDtypeStruct((8, tokens), jnp.int32),
        ],
        in_specs=[whole] * 3,
        out_specs=[pl.BlockSpec(memory_space=pltpu.SMEM), whole],
        scratch_shapes=[
            pltpu.VMEM((n, 8, tokens), jnp.int32),
            pltpu.VMEM((8, tokens), jnp.int32),
            pltpu.SemaphoreType.DMA((n,)),
            pltpu.SemaphoreType.DMA((n,)),
        ],
        compiler_params=pltpu.CompilerParams(collective_id=0, has_side_effects=True),
    )(keep, match, weight)


def merge_kernel(
    side,
    info,
    keep_ref,
    match_ref,
    weight_ref,
    next_ref,
    gain_ref,
    frame_ref,
    after_ref,
    first_ref,
    outer_ref,
    own_ref,
    inner_ref,
    window,
    own_row,
    inc_row,
    inc_part,
    inc_weight,
    sems,
):
    count, groups = keep_ref.shape
    tokens = match_ref.shape[1]
    per = tokens // groups
    width = gain_ref.shape[1]
    kept_dev = own_ref.shape[0]
    edge = side // TILE
    tiles = (2 * side + kept_dev) // TILE
    f = pl.program_id(0)
    odd = info[count + 4]

    @pl.when(f == 0)
    def _():
        keep = keep_ref[...].astype(jnp.bfloat16)
        g = lax.broadcasted_iota(jnp.int32, (groups, tokens), 0)
        t_group = lax.broadcasted_iota(jnp.int32, (groups, tokens), 1) // per
        below = (g < t_group).astype(jnp.bfloat16)
        same = (g == t_group).astype(jnp.bfloat16)
        before = jnp.dot(keep, below, preferred_element_type=jnp.float32)
        kept = jnp.dot(keep, same, preferred_element_type=jnp.float32)
        own_row[...] = jnp.where(kept > 0.5, before.astype(jnp.int32), -10000)
        at = lax.broadcasted_iota(jnp.int32, (groups, groups), 0)
        other = lax.broadcasted_iota(jnp.int32, (groups, groups), 1)
        column = lax.dot_general(
            (other < at).astype(jnp.bfloat16),
            keep,
            (((1,), (1,)), ((), ())),
            preferred_element_type=jnp.float32,
        )
        for k in range(count):
            if k + 1 < count:
                target = match_ref[k + 1 : k + 2, :]
                inc_weight[k : k + 1, :] = weight_ref[k + 1 : k + 2, :]
            else:
                target = next_ref[0:1, :]
                inc_weight[k : k + 1, :] = next_ref[1:2, :]
            place = jnp.sum(
                jnp.where(g == target // per, column[:, k : k + 1], 0.0), axis=0, keepdims=True
            )
            inc_row[k : k + 1, :] = jnp.where(target >= 0, place.astype(jnp.int32), -10000)
            inc_part[k : k + 1, :] = target % per

    start = info[f]
    base = pl.multiple_of((start // TILE) * TILE, TILE)
    off = start - base
    need = info[f + 1] - base

    def work(later_ref, rows):
        line = lax.broadcasted_iota(jnp.int32, (per * rows, tokens), 0)
        part = lax.broadcasted_iota(jnp.int32, (1, tokens), 1) % per
        own_key = own_row[pl.ds(f, 1), :] + off + part * rows
        inc_key = inc_row[pl.ds(f, 1), :] + off + inc_part[pl.ds(f, 1), :] * rows
        mine = jnp.where(line == own_key, weight_ref[pl.ds(f, 1), :].astype(jnp.float32), 0.0)
        theirs = jnp.where(line == inc_key, inc_weight[pl.ds(f, 1), :].astype(jnp.float32), 0.0)
        total = jnp.maximum(jnp.sum(mine + theirs, axis=1, keepdims=True), 1.0)
        summed = jnp.dot(
            mine.astype(jnp.bfloat16), frame_ref[0], preferred_element_type=jnp.float32
        ) + jnp.dot(theirs.astype(jnp.bfloat16), later_ref[0], preferred_element_type=jnp.float32)
        mean = jnp.sum(summed * summed, axis=1, keepdims=True) * (1.0 / width)
        scale = lax.rsqrt(mean + 1e-06 * total * total)
        normed = summed * scale * gain_ref[...]
        old_rows = lax.broadcasted_iota(jnp.int32, (TILE, width), 0) < off
        for j in range(per):
            cols = slice(j * width, (j + 1) * width)
            old = window[pl.ds(base, TILE), cols].astype(jnp.float32)
            head = jnp.where(old_rows, old, normed[j * rows : j * rows + TILE])
            window[pl.ds(base, TILE), cols] = head.astype(jnp.bfloat16)
            window[pl.ds(pl.multiple_of(base + TILE, TILE), rows - TILE), cols] = normed[
                j * rows + TILE : (j + 1) * rows
            ].astype(jnp.bfloat16)

    last = f == count - 1

    @pl.when(jnp.logical_not(last) & (need <= 48))
    def _():
        work(after_ref, 48)

    @pl.when(jnp.logical_not(last) & (need > 48) & (need <= 64))
    def _():
        work(after_ref, 64)

    @pl.when(jnp.logical_not(last) & (need > 64))
    def _():
        work(after_ref, groups + TILE)

    @pl.when(last)
    def _():
        work(first_ref, groups + TILE)

    def send(tile, target, place):
        pltpu.make_async_copy(
            window.at[pl.ds(pl.multiple_of(tile * TILE, TILE), TILE)],
            target.at[pl.ds(pl.multiple_of(place * TILE, TILE), TILE)],
            sems.at[tile],
        ).start()

    def flush(tile, carry):
        top = tile < edge
        end = tile >= tiles - edge

        @pl.when(top & (odd == 0))
        def _():
            send(tile, outer_ref, tile)

        @pl.when(top & (odd == 1))
        def _():
            send(tile, inner_ref, tile)

        @pl.when(jnp.logical_not(top | end))
        def _():
            send(tile, own_ref, tile - edge)

        @pl.when(end & (odd == 0))
        def _():
            send(tile, inner_ref, tile - (tiles - edge))

        @pl.when(end & (odd == 1))
        def _():
            send(tile, outer_ref, tile - (tiles - edge))

        return carry

    lax.fori_loop(
        jnp.where(f == 0, 0, start // TILE),
        jnp.where(last, tiles, info[f + 1] // TILE),
        flush,
        0,
    )

    @pl.when(last)
    def _():
        for tile in range(tiles):
            pltpu.make_async_copy(
                window.at[pl.ds(tile * TILE, TILE)], own_ref.at[pl.ds(0, TILE)], sems.at[tile]
            ).wait()


def merge(info, keep, match, weight, after, gain, frames, first, side, kept_dev):
    count, tokens, width = frames.shape
    groups = keep.shape[1]
    row = tokens // groups * width
    whole = pl.BlockSpec(memory_space=pltpu.VMEM)
    return pl.pallas_call(
        functools.partial(merge_kernel, side),
        out_shape=[
            jax.ShapeDtypeStruct((side, row), jnp.bfloat16),
            jax.ShapeDtypeStruct((kept_dev, row), jnp.bfloat16),
            jax.ShapeDtypeStruct((side, row), jnp.bfloat16),
        ],
        grid_spec=pltpu.PrefetchScalarGridSpec(
            num_scalar_prefetch=1,
            grid=(count,),
            in_specs=[
                whole,
                whole,
                whole,
                whole,
                whole,
                pl.BlockSpec((1, tokens, width), lambda f, s: (f, 0, 0)),
                pl.BlockSpec((1, tokens, width), lambda f, s: (jnp.minimum(f + 1, count - 1), 0, 0)),
                pl.BlockSpec((1, tokens, width), lambda f, s: (0, 0, 0)),
            ],
            out_specs=[pl.BlockSpec(memory_space=pl.ANY)] * 3,
            scratch_shapes=[
                pltpu.VMEM((2 * side + kept_dev + groups + TILE, row), jnp.bfloat16),
                pltpu.VMEM((count, tokens), jnp.int32),
                pltpu.VMEM((count, tokens), jnp.int32),
                pltpu.VMEM((count, tokens), jnp.int32),
                pltpu.VMEM((count, tokens), jnp.int32),
                pltpu.SemaphoreType.DMA(((2 * side + kept_dev) // TILE,)),
            ],
        ),
        compiler_params=pltpu.CompilerParams(vmem_limit_bytes=48 * 1024 * 1024),
    )(info, keep, match, weight, after, gain, frames, frames, first)


def finish_kernel(side, count, info, own_ref, inner_ref, outer_ref, out_ref):
    block = own_ref.shape[0]
    i = pl.program_id(0)
    row = i * block + lax.broadcasted_iota(jnp.int32, own_ref.shape, 0)
    even = info[count + 4] == 0
    here = info[count + 1]
    later = info[count + 2]
    kept_dev = pl.num_programs(0) * block
    top = i * block < here
    bottom = (i + 1) * block > kept_dev + later

    def mix(source):
        mask = (row < here) | (row >= kept_dev + later)
        mixed = jnp.where(
            mask, source[...].astype(jnp.float32), own_ref[...].astype(jnp.float32)
        )
        out_ref[...] = mixed.astype(out_ref.dtype)

    @pl.when((top & even) | (bottom & jnp.logical_not(even)))
    def _():
        mix(outer_ref)

    @pl.when((top & jnp.logical_not(even)) | (bottom & even))
    def _():
        mix(inner_ref)

    @pl.when(jnp.logical_not(top | bottom))
    def _():
        out_ref[...] = own_ref[...]


def finish(info, own, inner, outer, count, chunk):
    kept_dev, row = own.shape
    side = inner.shape[0]
    steps = kept_dev // chunk
    inner_blocks = side // chunk
    outer_blocks = outer.shape[0] // chunk

    def place(blocks, at_top):
        def index(i, info):
            start = jnp.where((info[count + 4] == 0) == at_top, 0, steps - blocks)
            return jnp.clip(i - start, 0, blocks - 1), 0

        return index

    return pl.pallas_call(
        functools.partial(finish_kernel, side, count),
        out_shape=jax.ShapeDtypeStruct(own.shape, own.dtype),
        grid_spec=pltpu.PrefetchScalarGridSpec(
            num_scalar_prefetch=1,
            grid=(steps,),
            in_specs=[
                pl.BlockSpec((chunk, row), lambda i, info: (i, 0)),
                pl.BlockSpec((chunk, row), place(inner_blocks, False)),
                pl.BlockSpec((chunk, row), place(outer_blocks, True)),
            ],
            out_specs=pl.BlockSpec((chunk, row), lambda i, info: (i, 0)),
        ),
        compiler_params=pltpu.CompilerParams(vmem_limit_bytes=32 * 1024 * 1024),
    )(info, own, inner, outer)


def body(frames, match, weight, keep, gain):
    count, tokens, width = frames.shape
    groups = keep.shape[1]
    kept_dev = count * groups // 2
    drift = kept_dev // 2 - count
    chunk = 2 * TILE
    side = -(-drift // chunk) * chunk
    n = lax.axis_size("seq")
    first = lax.ppermute(frames[:1], "seq", [(i + 1, i) for i in range(n - 1)])
    info, after = exchange(keep, match, weight, side, chunk)
    outer, own, inner = merge(
        info, keep, match, weight, after, gain.reshape(1, width), frames, first, side, kept_dev
    )
    inner = lax.ppermute(inner, "seq", [(i, i ^ 1) for i in range(n)])
    onward = [(i, i + 1) for i in range(1, n - 1, 2)]
    backward = [(j, i) for i, j in onward]

    def still(outer, own, inner):
        return finish(info, own, inner, outer, count, chunk)

    def forth(rows):
        def run(outer, own, inner):
            return finish(info, own, inner, lax.ppermute(outer[:rows], "seq", onward), count, chunk)

        return run

    def back(rows):
        def run(outer, own, inner):
            moved = lax.ppermute(outer[side - rows :], "seq", backward)
            return finish(info, own, inner, moved, count, chunk)

        return run

    sizes = range(chunk, side + 1, chunk)
    branches = [still] + [forth(rows) for rows in sizes] + [back(rows) for rows in sizes]
    return lax.switch(info[count + 3], branches, outer, own, inner)


def solution(mesh):
    placed = (
        P(("groups", "seq"), None, None),
        P(("groups", "seq"), None),
        P(("groups", "seq"), None),
        P(("groups", "seq"), None),
        P(),
    )
    return jax.shard_map(
        body, mesh=mesh, in_specs=placed, out_specs=P(("groups", "seq"), None), check_vma=False
    )
```

```python
import functools

import jax
import jax.numpy as jnp
from jax import lax
from jax.experimental import pallas as pl
from jax.experimental.pallas import tpu as pltpu
from jax.sharding import PartitionSpec as P

TILE = 16


def exchange_kernel(
    n,
    side,
    chunk,
    keep_ref,
    match_ref,
    weight_ref,
    frames_ref,
    info_ref,
    table_ref,
    first_ref,
    everyone,
    own,
    send_sem,
    recv_sem,
    frame_sems,
):
    count, groups = keep_ref.shape
    tokens = match_ref.shape[1]
    per = tokens // groups
    kept_dev = count * groups // 2
    me = lax.axis_index("seq")
    barrier = pltpu.get_barrier_semaphore()

    def greet(step, carry):
        peer = lax.rem(me + step, n)
        pl.semaphore_signal(
            barrier, inc=1, device_id={"seq": peer}, device_id_type=pl.DeviceIdType.MESH
        )
        return carry

    lax.fori_loop(1, n, greet, 0)
    keep = keep_ref[...].astype(jnp.float32)
    own[0:1, :] = match_ref[0:1, :]
    own[1:2, :] = weight_ref[0:1, :]
    total = jnp.sum(keep, keepdims=True).astype(jnp.int32)
    own[2:8, :] = jnp.broadcast_to(total, (6, tokens))
    everyone[pl.ds(me, 1)] = own[...][None]
    pl.semaphore_wait(barrier, n - 1)

    def copy(step):
        peer = lax.rem(me + step, n)
        return pltpu.make_async_remote_copy(
            src_ref=own,
            dst_ref=everyone.at[me],
            send_sem=send_sem.at[step],
            recv_sem=recv_sem.at[step],
            device_id={"seq": peer},
            device_id_type=pl.DeviceIdType.MESH,
        )

    def send(step, carry):
        copy(step).start()
        return carry

    def finish(step, carry):
        copy(step).wait()
        return carry

    lax.fori_loop(1, n, send, 0)
    frame_copy = pltpu.make_async_remote_copy(
        src_ref=frames_ref.at[pl.ds(0, 1)],
        dst_ref=first_ref,
        send_sem=frame_sems.at[0],
        recv_sem=frame_sems.at[1],
        device_id={"seq": lax.rem(me + n - 1, n)},
        device_id_type=pl.DeviceIdType.MESH,
    )
    stand_in = pltpu.make_async_copy(frames_ref.at[pl.ds(0, 1)], first_ref, frame_sems.at[2])

    @pl.when(me > 0)
    def _():
        frame_copy.start()

    @pl.when(me == n - 1)
    def _():
        stand_in.start()

    frame = lax.broadcasted_iota(jnp.int32, keep.shape, 0)
    earlier = [
        jnp.sum(jnp.where(frame < f, keep, 0.0)).astype(jnp.int32) for f in range(count + 1)
    ]
    kept_bits = keep.astype(jnp.bfloat16)
    g = lax.broadcasted_iota(jnp.int32, (groups, tokens), 0)
    t_group = lax.broadcasted_iota(jnp.int32, (groups, tokens), 1) // per
    below = (g < t_group).astype(jnp.bfloat16)
    same = (g == t_group).astype(jnp.bfloat16)
    before = jnp.dot(kept_bits, below, preferred_element_type=jnp.float32)
    kept = jnp.dot(kept_bits, same, preferred_element_type=jnp.float32)
    table_ref[0] = jnp.where(kept > 0.5, before.astype(jnp.int32), -10000)
    table_ref[4] = weight_ref[...]
    at = lax.broadcasted_iota(jnp.int32, (groups, groups), 0)
    other = lax.broadcasted_iota(jnp.int32, (groups, groups), 1)
    column = lax.dot_general(
        (other < at).astype(jnp.bfloat16),
        kept_bits,
        (((1,), (1,)), ((), ())),
        preferred_element_type=jnp.float32,
    )

    def incoming(k, target, heavy):
        place = jnp.sum(
            jnp.where(g == target // per, column[:, k : k + 1], 0.0), axis=0, keepdims=True
        )
        table_ref[1, k : k + 1, :] = jnp.where(target >= 0, place.astype(jnp.int32), -10000)
        table_ref[2, k : k + 1, :] = target % per
        table_ref[3, k : k + 1, :] = heavy

    for k in range(count - 1):
        incoming(k, match_ref[k + 1 : k + 2, :], weight_ref[k + 1 : k + 2, :])
    lax.fori_loop(1, n, finish, 0)
    counts = (everyone[:, 2, :] - kept_dev).astype(jnp.float32)
    device = lax.broadcasted_iota(jnp.int32, counts.shape, 0)
    lane = lax.broadcasted_iota(jnp.int32, counts.shape, 1)
    counts = jnp.where(lane == 0, counts, 0.0)
    here = jnp.sum(jnp.where(device < me, counts, 0.0)).astype(jnp.int32)
    later = jnp.sum(jnp.where(device <= me, counts, 0.0)).astype(jnp.int32)
    for f in range(count + 1):
        info_ref[f] = earlier[f] + (here + side)
    odd = lax.rem(me, 2)
    outer = jnp.where(odd == 1, later, here)
    pieces = (jnp.abs(outer) + (chunk - 1)) // chunk
    info_ref[count + 1] = here
    info_ref[count + 2] = later
    info_ref[count + 3] = jnp.where(outer < 0, pieces + side // chunk, pieces)
    info_ref[count + 4] = odd
    block = everyone[jnp.minimum(me + 1, n - 1)]
    incoming(count - 1, block[0:1, :], jnp.where(me == n - 1, 0, block[1:2, :]))

    @pl.when(me > 0)
    def _():
        frame_copy.wait_send()

    @pl.when(me < n - 1)
    def _():
        frame_copy.wait_recv()

    @pl.when(me == n - 1)
    def _():
        stand_in.wait()


def exchange(keep, match, weight, frames, side, chunk):
    n = lax.axis_size("seq")
    count, tokens = match.shape
    whole = pl.BlockSpec(memory_space=pltpu.VMEM)
    return pl.pallas_call(
        functools.partial(exchange_kernel, n, side, chunk),
        out_shape=[
            jax.ShapeDtypeStruct((count + 5,), jnp.int32),
            jax.ShapeDtypeStruct((5, count, tokens), jnp.int32),
            jax.ShapeDtypeStruct((1,) + frames.shape[1:], frames.dtype),
        ],
        in_specs=[whole] * 3 + [pl.BlockSpec(memory_space=pl.ANY)],
        out_specs=[
            pl.BlockSpec(memory_space=pltpu.SMEM),
            whole,
            pl.BlockSpec(memory_space=pl.ANY),
        ],
        scratch_shapes=[
            pltpu.VMEM((n, 8, tokens), jnp.int32),
            pltpu.VMEM((8, tokens), jnp.int32),
            pltpu.SemaphoreType.DMA((n,)),
            pltpu.SemaphoreType.DMA((n,)),
            pltpu.SemaphoreType.DMA((3,)),
        ],
        compiler_params=pltpu.CompilerParams(collective_id=0, has_side_effects=True),
    )(keep, match, weight, frames)


def merge_kernel(
    side,
    info,
    table_ref,
    gain_ref,
    frame_ref,
    after_ref,
    first_ref,
    outer_ref,
    own_ref,
    inner_ref,
    window,
    sems,
):
    count = table_ref.shape[1]
    batch, tokens, width = frame_ref.shape
    per = own_ref.shape[1] // width
    groups = tokens // per
    kept_dev = own_ref.shape[0]
    edge = side // TILE
    tiles = (2 * side + kept_dev) // TILE
    f = pl.program_id(0)
    odd = info[count + 4]
    last = f == pl.num_programs(0) - 1
    lead = f * batch
    starts = [info[lead + k] for k in range(batch + 1)]
    bases = [pl.multiple_of((start // TILE) * TILE, TILE) for start in starts[:-1]]
    need = starts[1] - bases[0]
    for k in range(1, batch):
        need = jnp.maximum(need, starts[k + 1] - bases[k])

    def work(rows):
        high = per * rows
        line = lax.broadcasted_iota(jnp.int32, (high, tokens), 0)
        part = lax.broadcasted_iota(jnp.int32, (1, tokens), 1) % per * rows
        ready = []
        for k in range(batch):
            at = pl.ds(lead + k, 1)
            off = starts[k] - bases[k]
            own_key = table_ref[0, at, :] + off + part
            inc_key = table_ref[1, at, :] + off + table_ref[2, at, :] * rows
            mine = jnp.where(line == own_key, table_ref[4, at, :].astype(jnp.float32), 0.0)
            theirs = jnp.where(line == inc_key, table_ref[3, at, :].astype(jnp.float32), 0.0)
            total = jnp.maximum(jnp.sum(mine + theirs, axis=1, keepdims=True), 1.0)
            if k + 1 < batch:
                later = frame_ref[k + 1]
            else:
                later = jnp.where(last, first_ref[0], after_ref[0])
            summed = jnp.dot(
                mine.astype(jnp.bfloat16), frame_ref[k], preferred_element_type=jnp.float32
            ) + jnp.dot(theirs.astype(jnp.bfloat16), later, preferred_element_type=jnp.float32)
            mean = jnp.sum(summed * summed, axis=1, keepdims=True) * (1.0 / width)
            scale = lax.rsqrt(mean + 1e-06 * total * total)
            ready.append(summed * scale * gain_ref[...])
        for k in range(batch):
            base = bases[k]
            normed = ready[k]
            old_rows = lax.broadcasted_iota(jnp.int32, (TILE, width), 0) < starts[k] - base
            for j in range(per):
                cols = slice(j * width, (j + 1) * width)
                old = window[pl.ds(base, TILE), cols].astype(jnp.float32)
                head = jnp.where(old_rows, old, normed[j * rows : j * rows + TILE])
                window[pl.ds(base, TILE), cols] = head.astype(jnp.bfloat16)
                window[pl.ds(pl.multiple_of(base + TILE, TILE), rows - TILE), cols] = normed[
                    j * rows + TILE : (j + 1) * rows
                ].astype(jnp.bfloat16)

    @pl.when(need <= 48)
    def _():
        work(48)

    @pl.when((need > 48) & (need <= 64))
    def _():
        work(64)

    @pl.when(need > 64)
    def _():
        work(groups + TILE)

    def send(tile, target, place):
        pltpu.make_async_copy(
            window.at[pl.ds(pl.multiple_of(tile * TILE, TILE), TILE)],
            target.at[pl.ds(pl.multiple_of(place * TILE, TILE), TILE)],
            sems.at[tile],
        ).start()

    def flush(tile, carry):
        top = tile < edge
        end = tile >= tiles - edge

        @pl.when(top & (odd == 0))
        def _():
            send(tile, outer_ref, tile)

        @pl.when(top & (odd == 1))
        def _():
            send(tile, inner_ref, tile)

        @pl.when(jnp.logical_not(top | end))
        def _():
            send(tile, own_ref, tile - edge)

        @pl.when(end & (odd == 0))
        def _():
            send(tile, inner_ref, tile - (tiles - edge))

        @pl.when(end & (odd == 1))
        def _():
            send(tile, outer_ref, tile - (tiles - edge))

        return carry

    lax.fori_loop(
        jnp.where(f == 0, 0, starts[0] // TILE),
        jnp.where(last, tiles, starts[batch] // TILE),
        flush,
        0,
    )

    @pl.when(last)
    def _():
        for tile in range(tiles):
            pltpu.make_async_copy(
                window.at[pl.ds(tile * TILE, TILE)], own_ref.at[pl.ds(0, TILE)], sems.at[tile]
            ).wait()


def merge(info, table, gain, frames, first, groups, side, kept_dev):
    count, tokens, width = frames.shape
    batch = 4 if count % 4 == 0 else 1
    row = tokens // groups * width
    whole = pl.BlockSpec(memory_space=pltpu.VMEM)
    return pl.pallas_call(
        functools.partial(merge_kernel, side),
        out_shape=[
            jax.ShapeDtypeStruct((side, row), jnp.bfloat16),
            jax.ShapeDtypeStruct((kept_dev, row), jnp.bfloat16),
            jax.ShapeDtypeStruct((side, row), jnp.bfloat16),
        ],
        grid_spec=pltpu.PrefetchScalarGridSpec(
            num_scalar_prefetch=1,
            grid=(count // batch,),
            in_specs=[
                whole,
                whole,
                pl.BlockSpec((batch, tokens, width), lambda f, s: (f, 0, 0)),
                pl.BlockSpec(
                    (1, tokens, width), lambda f, s: (jnp.minimum((f + 1) * batch, count - 1), 0, 0)
                ),
                pl.BlockSpec((1, tokens, width), lambda f, s: (0, 0, 0)),
            ],
            out_specs=[pl.BlockSpec(memory_space=pl.ANY)] * 3,
            scratch_shapes=[
                pltpu.VMEM((2 * side + kept_dev + groups + TILE, row), jnp.bfloat16),
                pltpu.SemaphoreType.DMA(((2 * side + kept_dev) // TILE,)),
            ],
        ),
        compiler_params=pltpu.CompilerParams(vmem_limit_bytes=60 * 1024 * 1024),
    )(info, table, gain, frames, frames, first)


def finish_kernel(side, count, info, own_ref, inner_ref, outer_ref, out_ref):
    block = own_ref.shape[0]
    i = pl.program_id(0)
    row = i * block + lax.broadcasted_iota(jnp.int32, own_ref.shape, 0)
    even = info[count + 4] == 0
    here = info[count + 1]
    later = info[count + 2]
    kept_dev = pl.num_programs(0) * block
    top = i * block < here
    bottom = (i + 1) * block > kept_dev + later

    def mix(source):
        mask = (row < here) | (row >= kept_dev + later)
        mixed = jnp.where(
            mask, source[...].astype(jnp.float32), own_ref[...].astype(jnp.float32)
        )
        out_ref[...] = mixed.astype(out_ref.dtype)

    @pl.when((top & even) | (bottom & jnp.logical_not(even)))
    def _():
        mix(outer_ref)

    @pl.when((top & jnp.logical_not(even)) | (bottom & even))
    def _():
        mix(inner_ref)

    @pl.when(jnp.logical_not(top | bottom))
    def _():
        out_ref[...] = own_ref[...]


def finish(info, own, inner, outer, count, chunk):
    kept_dev, row = own.shape
    side = inner.shape[0]
    steps = kept_dev // chunk
    inner_blocks = side // chunk
    outer_blocks = outer.shape[0] // chunk

    def place(blocks, at_top):
        def index(i, info):
            start = jnp.where((info[count + 4] == 0) == at_top, 0, steps - blocks)
            return jnp.clip(i - start, 0, blocks - 1), 0

        return index

    return pl.pallas_call(
        functools.partial(finish_kernel, side, count),
        out_shape=jax.ShapeDtypeStruct(own.shape, own.dtype),
        grid_spec=pltpu.PrefetchScalarGridSpec(
            num_scalar_prefetch=1,
            grid=(steps,),
            in_specs=[
                pl.BlockSpec((chunk, row), lambda i, info: (i, 0)),
                pl.BlockSpec((chunk, row), place(inner_blocks, False)),
                pl.BlockSpec((chunk, row), place(outer_blocks, True)),
            ],
            out_specs=pl.BlockSpec((chunk, row), lambda i, info: (i, 0)),
        ),
        compiler_params=pltpu.CompilerParams(vmem_limit_bytes=60 * 1024 * 1024),
    )(info, own, inner, outer)


def body(frames, match, weight, keep, gain):
    count, tokens, width = frames.shape
    groups = keep.shape[1]
    kept_dev = count * groups // 2
    drift = kept_dev // 2 - count
    chunk = 2 * TILE
    side = -(-drift // chunk) * chunk
    n = lax.axis_size("seq")
    info, table, first = exchange(keep, match, weight, frames, side, chunk)
    outer, own, inner = merge(
        info, table, gain.reshape(1, width), frames, first, groups, side, kept_dev
    )
    inner = lax.ppermute(inner, "seq", [(i, i ^ 1) for i in range(n)])
    onward = [(i, i + 1) for i in range(1, n - 1, 2)]
    backward = [(j, i) for i, j in onward]

    def still(outer, own, inner):
        return finish(info, own, inner, outer, count, chunk)

    def forth(rows):
        def run(outer, own, inner):
            return finish(info, own, inner, lax.ppermute(outer[:rows], "seq", onward), count, chunk)

        return run

    def back(rows):
        def run(outer, own, inner):
            moved = lax.ppermute(outer[side - rows :], "seq", backward)
            return finish(info, own, inner, moved, count, chunk)

        return run

    sizes = range(chunk, side + 1, chunk)
    branches = [still] + [forth(rows) for rows in sizes] + [back(rows) for rows in sizes]
    return lax.switch(info[count + 3], branches, outer, own, inner)


def solution(mesh):
    placed = (
        P(("groups", "seq"), None, None),
        P(("groups", "seq"), None),
        P(("groups", "seq"), None),
        P(("groups", "seq"), None),
        P(),
    )
    return jax.shard_map(
        body, mesh=mesh, in_specs=placed, out_specs=P(("groups", "seq"), None), check_vma=False
    )
```

```python
import functools

import jax
import jax.numpy as jnp
from jax import lax
from jax.experimental import pallas as pl
from jax.experimental.pallas import tpu as pltpu
from jax.sharding import PartitionSpec as P

TILE = 16


def exchange_kernel(
    n,
    side,
    chunk,
    keep_ref,
    match_ref,
    weight_ref,
    frames_ref,
    info_ref,
    table_ref,
    first_ref,
    everyone,
    own,
    send_sem,
    recv_sem,
    frame_sems,
):
    count, groups = keep_ref.shape
    tokens = match_ref.shape[1]
    per = tokens // groups
    kept_dev = count * groups // 2
    me = lax.axis_index("seq")
    barrier = pltpu.get_barrier_semaphore()

    def greet(step, carry):
        peer = lax.rem(me + step, n)
        pl.semaphore_signal(
            barrier, inc=1, device_id={"seq": peer}, device_id_type=pl.DeviceIdType.MESH
        )
        return carry

    lax.fori_loop(1, n, greet, 0)
    keep = keep_ref[...].astype(jnp.float32)
    own[0:1, :] = match_ref[0:1, :]
    own[1:2, :] = weight_ref[0:1, :]
    total = jnp.sum(keep, keepdims=True).astype(jnp.int32)
    own[2:8, :] = jnp.broadcast_to(total, (6, tokens))
    everyone[pl.ds(me, 1)] = own[...][None]
    pl.semaphore_wait(barrier, n - 1)

    def copy(step):
        peer = lax.rem(me + step, n)
        return pltpu.make_async_remote_copy(
            src_ref=own,
            dst_ref=everyone.at[me],
            send_sem=send_sem.at[step],
            recv_sem=recv_sem.at[step],
            device_id={"seq": peer},
            device_id_type=pl.DeviceIdType.MESH,
        )

    def send(step, carry):
        copy(step).start()
        return carry

    def finish(step, carry):
        copy(step).wait()
        return carry

    lax.fori_loop(1, n, send, 0)
    frame_copy = pltpu.make_async_remote_copy(
        src_ref=frames_ref.at[pl.ds(0, 1)],
        dst_ref=first_ref,
        send_sem=frame_sems.at[0],
        recv_sem=frame_sems.at[1],
        device_id={"seq": lax.rem(me + n - 1, n)},
        device_id_type=pl.DeviceIdType.MESH,
    )
    @pl.when(me > 0)
    def _():
        frame_copy.start()

    frame = lax.broadcasted_iota(jnp.int32, keep.shape, 0)
    earlier = [
        jnp.sum(jnp.where(frame < f, keep, 0.0)).astype(jnp.int32) for f in range(count + 1)
    ]
    kept_bits = keep.astype(jnp.bfloat16)
    g = lax.broadcasted_iota(jnp.int32, (groups, tokens), 0)
    t_group = lax.broadcasted_iota(jnp.int32, (groups, tokens), 1) // per
    below = (g < t_group).astype(jnp.bfloat16)
    same = (g == t_group).astype(jnp.bfloat16)
    before = jnp.dot(kept_bits, below, preferred_element_type=jnp.float32)
    kept = jnp.dot(kept_bits, same, preferred_element_type=jnp.float32)
    table_ref[0] = jnp.where(kept > 0.5, before.astype(jnp.int32), -10000)
    table_ref[4] = weight_ref[...]
    at = lax.broadcasted_iota(jnp.int32, (groups, groups), 0)
    other = lax.broadcasted_iota(jnp.int32, (groups, groups), 1)
    column = lax.dot_general(
        (other < at).astype(jnp.bfloat16),
        kept_bits,
        (((1,), (1,)), ((), ())),
        preferred_element_type=jnp.float32,
    )

    def incoming(k, target, heavy):
        place = jnp.sum(
            jnp.where(g == target // per, column[:, k : k + 1], 0.0), axis=0, keepdims=True
        )
        table_ref[1, k : k + 1, :] = jnp.where(target >= 0, place.astype(jnp.int32), -10000)
        table_ref[2, k : k + 1, :] = target % per
        table_ref[3, k : k + 1, :] = heavy

    for k in range(count - 1):
        incoming(k, match_ref[k + 1 : k + 2, :], weight_ref[k + 1 : k + 2, :])
    lax.fori_loop(1, n, finish, 0)
    counts = (everyone[:, 2, :] - kept_dev).astype(jnp.float32)
    device = lax.broadcasted_iota(jnp.int32, counts.shape, 0)
    lane = lax.broadcasted_iota(jnp.int32, counts.shape, 1)
    counts = jnp.where(lane == 0, counts, 0.0)
    here = jnp.sum(jnp.where(device < me, counts, 0.0)).astype(jnp.int32)
    later = jnp.sum(jnp.where(device <= me, counts, 0.0)).astype(jnp.int32)
    for f in range(count + 1):
        info_ref[f] = earlier[f] + (here + side)
    odd = lax.rem(me, 2)
    outer = jnp.where(odd == 1, later, here)
    pieces = (jnp.abs(outer) + (chunk - 1)) // chunk
    info_ref[count + 1] = here
    info_ref[count + 2] = later
    info_ref[count + 3] = jnp.where(outer < 0, pieces + side // chunk, pieces)
    info_ref[count + 4] = odd
    info_ref[count + 5] = jnp.where(me == n - 1, 1, 0)
    block = everyone[jnp.minimum(me + 1, n - 1)]
    incoming(count - 1, block[0:1, :], jnp.where(me == n - 1, 0, block[1:2, :]))

    @pl.when(me > 0)
    def _():
        frame_copy.wait_send()

    @pl.when(me < n - 1)
    def _():
        frame_copy.wait_recv()


def exchange(keep, match, weight, frames, side, chunk):
    n = lax.axis_size("seq")
    count, tokens = match.shape
    whole = pl.BlockSpec(memory_space=pltpu.VMEM)
    return pl.pallas_call(
        functools.partial(exchange_kernel, n, side, chunk),
        out_shape=[
            jax.ShapeDtypeStruct((count + 6,), jnp.int32),
            jax.ShapeDtypeStruct((5, count, tokens), jnp.int32),
            jax.ShapeDtypeStruct((1,) + frames.shape[1:], frames.dtype),
        ],
        in_specs=[whole] * 3 + [pl.BlockSpec(memory_space=pl.ANY)],
        out_specs=[
            pl.BlockSpec(memory_space=pltpu.SMEM),
            whole,
            pl.BlockSpec(memory_space=pl.ANY),
        ],
        scratch_shapes=[
            pltpu.VMEM((n, 8, tokens), jnp.int32),
            pltpu.VMEM((8, tokens), jnp.int32),
            pltpu.SemaphoreType.DMA((n,)),
            pltpu.SemaphoreType.DMA((n,)),
            pltpu.SemaphoreType.DMA((2,)),
        ],
        compiler_params=pltpu.CompilerParams(collective_id=0, has_side_effects=True),
    )(keep, match, weight, frames)


def merge_kernel(
    side,
    info,
    table_ref,
    gain_ref,
    frame_ref,
    after_ref,
    first_ref,
    outer_ref,
    own_ref,
    inner_ref,
    window,
    sems,
):
    count = table_ref.shape[1]
    batch, tokens, width = frame_ref.shape
    per = own_ref.shape[1] // width
    groups = tokens // per
    kept_dev = own_ref.shape[0]
    edge = side // TILE
    tiles = (2 * side + kept_dev) // TILE
    f = pl.program_id(0)
    odd = info[count + 4]
    last = f == pl.num_programs(0) - 1
    lead = f * batch
    starts = [info[lead + k] for k in range(batch + 1)]
    bases = [pl.multiple_of((start // TILE) * TILE, TILE) for start in starts[:-1]]
    need = starts[1] - bases[0]
    for k in range(1, batch):
        need = jnp.maximum(need, starts[k + 1] - bases[k])

    def work(rows):
        high = per * rows
        line = lax.broadcasted_iota(jnp.int32, (high, tokens), 0)
        part = lax.broadcasted_iota(jnp.int32, (1, tokens), 1) % per * rows
        ready = []
        for k in range(batch):
            at = pl.ds(lead + k, 1)
            off = starts[k] - bases[k]
            own_key = table_ref[0, at, :] + off + part
            inc_key = table_ref[1, at, :] + off + table_ref[2, at, :] * rows
            mine = jnp.where(line == own_key, table_ref[4, at, :].astype(jnp.float32), 0.0)
            theirs = jnp.where(line == inc_key, table_ref[3, at, :].astype(jnp.float32), 0.0)
            total = jnp.maximum(jnp.sum(mine + theirs, axis=1, keepdims=True), 1.0)
            if k + 1 < batch:
                later = frame_ref[k + 1]
            else:
                end = jnp.where(info[count + 5] == 1, jnp.zeros_like(first_ref[0]), first_ref[0])
                later = jnp.where(last, end, after_ref[0])
            summed = jnp.dot(
                mine.astype(jnp.bfloat16), frame_ref[k], preferred_element_type=jnp.float32
            ) + jnp.dot(theirs.astype(jnp.bfloat16), later, preferred_element_type=jnp.float32)
            mean = jnp.sum(summed * summed, axis=1, keepdims=True) * (1.0 / width)
            scale = lax.rsqrt(mean + 1e-06 * total * total)
            ready.append(summed * scale * gain_ref[...][None, :])
        for k in range(batch):
            base = bases[k]
            normed = ready[k]
            old_rows = lax.broadcasted_iota(jnp.int32, (TILE, width), 0) < starts[k] - base
            for j in range(per):
                cols = slice(j * width, (j + 1) * width)
                old = window[pl.ds(base, TILE), cols].astype(jnp.float32)
                head = jnp.where(old_rows, old, normed[j * rows : j * rows + TILE])
                window[pl.ds(base, TILE), cols] = head.astype(jnp.bfloat16)
                window[pl.ds(pl.multiple_of(base + TILE, TILE), rows - TILE), cols] = normed[
                    j * rows + TILE : (j + 1) * rows
                ].astype(jnp.bfloat16)

    @pl.when(need <= 48)
    def _():
        work(48)

    @pl.when((need > 48) & (need <= 64))
    def _():
        work(64)

    @pl.when(need > 64)
    def _():
        work(groups + TILE)

    def send(tile, target, place):
        pltpu.make_async_copy(
            window.at[pl.ds(pl.multiple_of(tile * TILE, TILE), TILE)],
            target.at[pl.ds(pl.multiple_of(place * TILE, TILE), TILE)],
            sems.at[tile],
        ).start()

    def flush(tile, carry):
        top = tile < edge
        end = tile >= tiles - edge

        @pl.when(top & (odd == 0))
        def _():
            send(tile, outer_ref, tile)

        @pl.when(top & (odd == 1))
        def _():
            send(tile, inner_ref, tile)

        @pl.when(jnp.logical_not(top | end))
        def _():
            send(tile, own_ref, tile - edge)

        @pl.when(end & (odd == 0))
        def _():
            send(tile, inner_ref, tile - (tiles - edge))

        @pl.when(end & (odd == 1))
        def _():
            send(tile, outer_ref, tile - (tiles - edge))

        return carry

    lax.fori_loop(
        jnp.where(f == 0, 0, starts[0] // TILE),
        jnp.where(last, tiles, starts[batch] // TILE),
        flush,
        0,
    )

    @pl.when(last)
    def _():
        for tile in range(tiles):
            pltpu.make_async_copy(
                window.at[pl.ds(tile * TILE, TILE)], own_ref.at[pl.ds(0, TILE)], sems.at[tile]
            ).wait()


def merge(info, table, gain, frames, first, groups, side, kept_dev):
    count, tokens, width = frames.shape
    batch = 4 if count % 4 == 0 else 1
    row = tokens // groups * width
    whole = pl.BlockSpec(memory_space=pltpu.VMEM)
    return pl.pallas_call(
        functools.partial(merge_kernel, side),
        out_shape=[
            jax.ShapeDtypeStruct((side, row), jnp.bfloat16),
            jax.ShapeDtypeStruct((kept_dev, row), jnp.bfloat16),
            jax.ShapeDtypeStruct((side, row), jnp.bfloat16),
        ],
        grid_spec=pltpu.PrefetchScalarGridSpec(
            num_scalar_prefetch=1,
            grid=(count // batch,),
            in_specs=[
                whole,
                whole,
                pl.BlockSpec((batch, tokens, width), lambda f, s: (f, 0, 0)),
                pl.BlockSpec(
                    (1, tokens, width), lambda f, s: (jnp.minimum((f + 1) * batch, count - 1), 0, 0)
                ),
                pl.BlockSpec((1, tokens, width), lambda f, s: (0, 0, 0)),
            ],
            out_specs=[pl.BlockSpec(memory_space=pl.ANY)] * 3,
            scratch_shapes=[
                pltpu.VMEM((2 * side + kept_dev + groups + TILE, row), jnp.bfloat16),
                pltpu.SemaphoreType.DMA(((2 * side + kept_dev) // TILE,)),
            ],
        ),
        compiler_params=pltpu.CompilerParams(vmem_limit_bytes=60 * 1024 * 1024),
    )(info, table, gain, frames, frames, first)


def finish_kernel(
    side, count, info, own_ref, inner_ref, outer_ref, out_ref, held, border, load_sems, edge_sems, save_sems
):
    tiles = side // TILE
    bottom_tile = (out_ref.shape[0] - side) // TILE
    here = info[count + 1]
    later = info[count + 2]
    even = info[count + 4] == 0
    tops = (jnp.maximum(here, 0) + (TILE - 1)) // TILE
    low = jnp.minimum(later, 0) + side
    low_tile = low // TILE
    spans = ((0, tops), (low_tile, tiles))
    places = (0, bottom_tile)
    edges = (tops - 1, low_tile)

    def rows(tile):
        return pl.ds(pl.multiple_of(tile * TILE, TILE), TILE)

    def load(half, tile, source):
        return pltpu.make_async_copy(
            source.at[rows(tile)], held.at[half, rows(tile)], load_sems.at[half, tile]
        )

    def save(half, tile):
        return pltpu.make_async_copy(
            held.at[half, rows(tile)],
            out_ref.at[rows(places[half] + tile)],
            save_sems.at[half, tile],
        )

    def old(half):
        return pltpu.make_async_copy(
            out_ref.at[rows(places[half] + edges[half])], border.at[half], edge_sems.at[half]
        )

    def start_load(half):
        def run(tile, carry):
            from_outer = even if half == 0 else jnp.logical_not(even)

            @pl.when(from_outer)
            def _():
                load(half, tile, outer_ref).start()

            @pl.when(jnp.logical_not(from_outer))
            def _():
                load(half, tile, inner_ref).start()

            return carry

        return run

    def end_load(half):
        def run(tile, carry):
            load(half, tile, outer_ref).wait()
            return carry

        return run

    def start_save(half):
        def run(tile, carry):
            save(half, tile).start()
            return carry

        return run

    def end_save(half):
        def run(tile, carry):
            save(half, tile).wait()
            return carry

        return run

    for half in (0, 1):
        low_end, high_end = spans[half]

        @pl.when(low_end < high_end)
        def _():
            old(half).start()
            lax.fori_loop(low_end, high_end, start_load(half), 0)

    for half in (0, 1):
        low_end, high_end = spans[half]

        @pl.when(low_end < high_end)
        def _():
            old(half).wait()
            lax.fori_loop(low_end, high_end, end_load(half), 0)
            row = lax.broadcasted_iota(jnp.int32, border.shape[1:], 0) + edges[half] * TILE
            new = row < here if half == 0 else row >= low
            at = rows(edges[half])
            mixed = jnp.where(
                new, held[half, at, :].astype(jnp.float32), border[half].astype(jnp.float32)
            )
            held[half, at, :] = mixed.astype(held.dtype)
            lax.fori_loop(low_end, high_end, start_save(half), 0)

    for half in (0, 1):
        lax.fori_loop(*spans[half], end_save(half), 0)


def finish(info, own, inner, outer, count):
    side, row = inner.shape
    hbm = pl.BlockSpec(memory_space=pl.ANY)
    return pl.pallas_call(
        functools.partial(finish_kernel, side, count),
        out_shape=jax.ShapeDtypeStruct(own.shape, own.dtype),
        in_specs=[pl.BlockSpec(memory_space=pltpu.SMEM), hbm, hbm, hbm],
        out_specs=hbm,
        input_output_aliases={1: 0},
        scratch_shapes=[
            pltpu.VMEM((2, side, row), own.dtype),
            pltpu.VMEM((2, TILE, row), own.dtype),
            pltpu.SemaphoreType.DMA((2, side // TILE)),
            pltpu.SemaphoreType.DMA((2,)),
            pltpu.SemaphoreType.DMA((2, side // TILE)),
        ],
        compiler_params=pltpu.CompilerParams(vmem_limit_bytes=60 * 1024 * 1024),
    )(info, own, inner, outer)


def body(frames, match, weight, keep, gain):
    count, tokens, width = frames.shape
    groups = keep.shape[1]
    kept_dev = count * groups // 2
    drift = kept_dev // 2 - count
    chunk = 2 * TILE
    side = -(-drift // chunk) * chunk
    n = lax.axis_size("seq")
    info, table, first = exchange(keep, match, weight, frames, side, chunk)
    outer, own, inner = merge(
        info, table, gain, frames, first, groups, side, kept_dev
    )
    inner = lax.ppermute(inner, "seq", [(i, i ^ 1) for i in range(n)])
    onward = [(i, i + 1) for i in range(1, n - 1, 2)]
    backward = [(j, i) for i, j in onward]

    def still(outer):
        return outer

    def forth(rows):
        def run(outer):
            moved = lax.ppermute(outer[:rows], "seq", onward)
            return jnp.pad(moved, ((0, side - rows), (0, 0)))

        return run

    def back(rows):
        def run(outer):
            moved = lax.ppermute(outer[side - rows :], "seq", backward)
            return jnp.pad(moved, ((side - rows, 0), (0, 0)))

        return run

    sizes = range(chunk, side + 1, chunk)
    branches = [still] + [forth(rows) for rows in sizes] + [back(rows) for rows in sizes]
    outer = lax.switch(info[count + 3], branches, outer)
    return finish(info, own, inner, outer, count)


def solution(mesh):
    placed = (
        P(("groups", "seq"), None, None),
        P(("groups", "seq"), None),
        P(("groups", "seq"), None),
        P(("groups", "seq"), None),
        P(),
    )
    return jax.shard_map(
        body, mesh=mesh, in_specs=placed, out_specs=P(("groups", "seq"), None), check_vma=False
    )
```

```python
import functools

import jax
import jax.numpy as jnp
from jax import lax
from jax.experimental import pallas as pl
from jax.experimental.pallas import tpu as pltpu
from jax.sharding import PartitionSpec as P

TILE = 16


def exchange_kernel(
    n,
    side,
    chunk,
    keep_ref,
    match_ref,
    weight_ref,
    frames_ref,
    info_ref,
    table_ref,
    head_ref,
    everyone,
    own,
    send_sem,
    recv_sem,
    head_sem,
):
    count, groups = keep_ref.shape
    tokens = match_ref.shape[1]
    per = tokens // groups
    kept_dev = count * groups // 2
    me = lax.axis_index("seq")
    barrier = pltpu.get_barrier_semaphore()

    def greet(step, carry):
        peer = lax.rem(me + step, n)
        pl.semaphore_signal(
            barrier, inc=1, device_id={"seq": peer}, device_id_type=pl.DeviceIdType.MESH
        )
        return carry

    lax.fori_loop(1, n, greet, 0)
    stage = pltpu.make_async_copy(frames_ref.at[pl.ds(0, 1)], head_ref, head_sem)
    stage.start()
    keep = keep_ref[...].astype(jnp.float32)
    own[0:1, :] = match_ref[0:1, :]
    own[1:2, :] = weight_ref[0:1, :]
    total = jnp.sum(keep, keepdims=True).astype(jnp.int32)
    own[2:8, :] = jnp.broadcast_to(total, (6, tokens))
    everyone[pl.ds(me, 1)] = own[...][None]
    kept_bits = keep.astype(jnp.bfloat16)
    g = lax.broadcasted_iota(jnp.int32, (groups, tokens), 0)
    t_group = lax.broadcasted_iota(jnp.int32, (groups, tokens), 1) // per
    below = (g < t_group).astype(jnp.bfloat16)
    same = (g == t_group).astype(jnp.bfloat16)
    before = jnp.dot(kept_bits, below, preferred_element_type=jnp.float32)
    kept = jnp.dot(kept_bits, same, preferred_element_type=jnp.float32)
    table_ref[0] = jnp.where(kept > 0.5, before.astype(jnp.int32), -10000)
    table_ref[4] = weight_ref[...]
    at = lax.broadcasted_iota(jnp.int32, (groups, groups), 0)
    other = lax.broadcasted_iota(jnp.int32, (groups, groups), 1)
    column = lax.dot_general(
        (other < at).astype(jnp.bfloat16),
        kept_bits,
        (((1,), (1,)), ((), ())),
        preferred_element_type=jnp.float32,
    )

    def incoming(k, target, heavy):
        place = jnp.sum(
            jnp.where(g == target // per, column[:, k : k + 1], 0.0), axis=0, keepdims=True
        )
        table_ref[1, k : k + 1, :] = jnp.where(target >= 0, place.astype(jnp.int32), -10000)
        table_ref[2, k : k + 1, :] = target % per
        table_ref[3, k : k + 1, :] = heavy

    for k in range(count - 1):
        incoming(k, match_ref[k + 1 : k + 2, :], weight_ref[k + 1 : k + 2, :])
    pl.semaphore_wait(barrier, n - 1)

    def copy(step):
        peer = lax.rem(me + step, n)
        return pltpu.make_async_remote_copy(
            src_ref=own,
            dst_ref=everyone.at[me],
            send_sem=send_sem.at[step],
            recv_sem=recv_sem.at[step],
            device_id={"seq": peer},
            device_id_type=pl.DeviceIdType.MESH,
        )

    def send(step, carry):
        copy(step).start()
        return carry

    def finish(step, carry):
        copy(step).wait()
        return carry

    lax.fori_loop(1, n, send, 0)
    frame = lax.broadcasted_iota(jnp.int32, keep.shape, 0)
    earlier = [
        jnp.sum(jnp.where(frame < f, keep, 0.0)).astype(jnp.int32) for f in range(count + 1)
    ]
    lax.fori_loop(1, n, finish, 0)
    counts = (everyone[:, 2, :] - kept_dev).astype(jnp.float32)
    device = lax.broadcasted_iota(jnp.int32, counts.shape, 0)
    lane = lax.broadcasted_iota(jnp.int32, counts.shape, 1)
    counts = jnp.where(lane == 0, counts, 0.0)
    here = jnp.sum(jnp.where(device < me, counts, 0.0)).astype(jnp.int32)
    later = jnp.sum(jnp.where(device <= me, counts, 0.0)).astype(jnp.int32)
    for f in range(count + 1):
        info_ref[f] = earlier[f] + (here + side)
    odd = lax.rem(me, 2)
    outer = jnp.where(odd == 1, later, here)
    pieces = (jnp.abs(outer) + (chunk - 1)) // chunk
    info_ref[count + 1] = here
    info_ref[count + 2] = later
    info_ref[count + 3] = jnp.where(outer < 0, pieces + side // chunk, pieces)
    info_ref[count + 4] = odd
    info_ref[count + 5] = jnp.where(me == n - 1, 1, 0)
    block = everyone[jnp.minimum(me + 1, n - 1)]
    incoming(count - 1, block[0:1, :], jnp.where(me == n - 1, 0, block[1:2, :]))

    stage.wait()


def exchange(keep, match, weight, frames, side, chunk):
    n = lax.axis_size("seq")
    count, tokens = match.shape
    whole = pl.BlockSpec(memory_space=pltpu.VMEM)
    return pl.pallas_call(
        functools.partial(exchange_kernel, n, side, chunk),
        out_shape=[
            jax.ShapeDtypeStruct((count + 6,), jnp.int32),
            jax.ShapeDtypeStruct((5, count, tokens), jnp.int32),
            jax.ShapeDtypeStruct((1,) + frames.shape[1:], frames.dtype),
        ],
        in_specs=[whole] * 3 + [pl.BlockSpec(memory_space=pl.ANY)],
        out_specs=[
            pl.BlockSpec(memory_space=pltpu.SMEM),
            whole,
            whole,
        ],
        scratch_shapes=[
            pltpu.VMEM((n, 8, tokens), jnp.int32),
            pltpu.VMEM((8, tokens), jnp.int32),
            pltpu.SemaphoreType.DMA((n,)),
            pltpu.SemaphoreType.DMA((n,)),
            pltpu.SemaphoreType.DMA(()),
        ],
        compiler_params=pltpu.CompilerParams(collective_id=0, has_side_effects=True),
    )(keep, match, weight, frames)


def merge_kernel(side, first_step, ends, info, table_ref, gain_ref, frame_ref, after_ref, *refs):
    if ends:
        first_ref, held_ref, _, _, _, outer_ref, own_ref, inner_ref, window, sems = refs
    else:
        first_ref = None
        outer_ref, own_ref, inner_ref, held_ref, window, sems = refs
    count = table_ref.shape[1]
    batch, tokens, width = frame_ref.shape
    per = own_ref.shape[1] // width
    groups = tokens // per
    kept_dev = own_ref.shape[0]
    edge = side // TILE
    tiles = (2 * side + kept_dev) // TILE
    f = pl.program_id(0)
    odd = info[count + 4]
    last = f == pl.num_programs(0) - 1
    lead = (f + first_step) * batch
    starts = [info[lead + k] for k in range(batch + 1)]
    bases = [pl.multiple_of((start // TILE) * TILE, TILE) for start in starts[:-1]]
    need = starts[1] - bases[0]
    for k in range(1, batch):
        need = jnp.maximum(need, starts[k + 1] - bases[k])

    def work(rows):
        high = per * rows
        line = lax.broadcasted_iota(jnp.int32, (high, tokens), 0)
        part = lax.broadcasted_iota(jnp.int32, (1, tokens), 1) % per * rows
        ready = []
        for k in range(batch):
            at = pl.ds(lead + k, 1)
            off = starts[k] - bases[k]
            own_key = table_ref[0, at, :] + off + part
            inc_key = table_ref[1, at, :] + off + table_ref[2, at, :] * rows
            mine = jnp.where(line == own_key, table_ref[4, at, :].astype(jnp.float32), 0.0)
            theirs = jnp.where(line == inc_key, table_ref[3, at, :].astype(jnp.float32), 0.0)
            total = jnp.maximum(jnp.sum(mine + theirs, axis=1, keepdims=True), 1.0)
            if k + 1 < batch:
                later = frame_ref[k + 1]
            else:
                later = after_ref[0]
                if ends:
                    end = jnp.where(info[count + 5] == 1, jnp.zeros_like(later), first_ref[0])
                    later = jnp.where(last, end, later)
            summed = jnp.dot(
                mine.astype(jnp.bfloat16), frame_ref[k], preferred_element_type=jnp.float32
            ) + jnp.dot(theirs.astype(jnp.bfloat16), later, preferred_element_type=jnp.float32)
            mean = jnp.sum(summed * summed, axis=1, keepdims=True) * (1.0 / width)
            scale = lax.rsqrt(mean + 1e-06 * total * total)
            ready.append(summed * scale * gain_ref[...][None, :])
        for k in range(batch):
            base = bases[k]
            normed = ready[k]
            old_rows = lax.broadcasted_iota(jnp.int32, (TILE, width), 0) < starts[k] - base
            for j in range(per):
                cols = slice(j * width, (j + 1) * width)
                old = window[pl.ds(base, TILE), cols].astype(jnp.float32)
                head = jnp.where(old_rows, old, normed[j * rows : j * rows + TILE])
                window[pl.ds(base, TILE), cols] = head.astype(jnp.bfloat16)
                window[pl.ds(pl.multiple_of(base + TILE, TILE), rows - TILE), cols] = normed[
                    j * rows + TILE : (j + 1) * rows
                ].astype(jnp.bfloat16)

    if ends:

        @pl.when(f == 0)
        def _():
            window[pl.ds(bases[0], TILE), :] = held_ref[...]

    @pl.when(need <= 48)
    def _():
        work(48)

    @pl.when((need > 48) & (need <= 64))
    def _():
        work(64)

    @pl.when(need > 64)
    def _():
        work(groups + TILE)

    def send(tile, target, place):
        pltpu.make_async_copy(
            window.at[pl.ds(pl.multiple_of(tile * TILE, TILE), TILE)],
            target.at[pl.ds(pl.multiple_of(place * TILE, TILE), TILE)],
            sems.at[tile],
        ).start()

    def flush(tile, carry):
        top = tile < edge
        end = tile >= tiles - edge

        @pl.when(top & (odd == 0))
        def _():
            send(tile, outer_ref, tile)

        @pl.when(top & (odd == 1))
        def _():
            send(tile, inner_ref, tile)

        @pl.when(jnp.logical_not(top | end))
        def _():
            send(tile, own_ref, tile - edge)

        @pl.when(end & (odd == 0))
        def _():
            send(tile, inner_ref, tile - (tiles - edge))

        @pl.when(end & (odd == 1))
        def _():
            send(tile, outer_ref, tile - (tiles - edge))

        return carry

    from_tile = info[first_step * batch] // TILE if ends else 0
    last_tile = tiles if ends else info[(first_step + pl.num_programs(0)) * batch] // TILE
    lax.fori_loop(
        jnp.where(f == 0, from_tile, starts[0] // TILE),
        jnp.where(last, last_tile, starts[batch] // TILE),
        flush,
        0,
    )

    @pl.when(last)
    def _():
        if not ends:
            held_ref[...] = window[pl.ds(pl.multiple_of(last_tile * TILE, TILE), TILE), :]

        def done(tile, carry):
            pltpu.make_async_copy(
                window.at[pl.ds(pl.multiple_of(tile * TILE, TILE), TILE)],
                own_ref.at[pl.ds(0, TILE)],
                sems.at[tile],
            ).wait()
            return carry

        lax.fori_loop(from_tile, last_tile, done, 0)


def merge(info, table, gain, frames, groups, side, kept_dev, batch, first_step, steps, late=None):
    count, tokens, width = frames.shape
    row = tokens // groups * width
    whole = pl.BlockSpec(memory_space=pltpu.VMEM)
    hbm = pl.BlockSpec(memory_space=pl.ANY)
    packed = [
        jax.ShapeDtypeStruct((side, row), jnp.bfloat16),
        jax.ShapeDtypeStruct((kept_dev, row), jnp.bfloat16),
        jax.ShapeDtypeStruct((side, row), jnp.bfloat16),
    ]
    in_specs = [
        whole,
        whole,
        pl.BlockSpec((batch, tokens, width), lambda f, s: (f + first_step, 0, 0)),
        pl.BlockSpec(
            (1, tokens, width),
            lambda f, s: (jnp.minimum((f + first_step + 1) * batch, count - 1), 0, 0),
        ),
    ]
    ends = late is not None
    operands = [info, table, gain, frames, frames]
    if ends:
        first, held, outer, own, inner = late
        in_specs += [whole, whole, hbm, hbm, hbm]
        operands += [first, held, outer, own, inner]
        out_shape, out_specs = packed, [hbm] * 3
        aliases = {7: 0, 8: 1, 9: 2}
    else:
        out_shape = packed + [jax.ShapeDtypeStruct((TILE, row), jnp.bfloat16)]
        out_specs = [hbm] * 3 + [whole]
        aliases = {}
    return pl.pallas_call(
        functools.partial(merge_kernel, side, first_step, ends),
        out_shape=out_shape,
        grid_spec=pltpu.PrefetchScalarGridSpec(
            num_scalar_prefetch=1,
            grid=(steps,),
            in_specs=in_specs,
            out_specs=out_specs,
            scratch_shapes=[
                pltpu.VMEM((2 * side + kept_dev + groups + TILE, row), jnp.bfloat16),
                pltpu.SemaphoreType.DMA(((2 * side + kept_dev) // TILE,)),
            ],
        ),
        input_output_aliases=aliases,
        cost_estimate=pl.CostEstimate(
            flops=10 * steps * batch * tokens * tokens * width,
            bytes_accessed=4 * steps * batch * tokens * width,
            transcendentals=0,
        ),
        compiler_params=pltpu.CompilerParams(vmem_limit_bytes=60 * 1024 * 1024),
    )(*operands)


def finish_kernel(
    side, count, info, own_ref, inner_ref, outer_ref, out_ref, held, border, load_sems, edge_sems, save_sems
):
    tiles = side // TILE
    bottom_tile = (out_ref.shape[0] - side) // TILE
    here = info[count + 1]
    later = info[count + 2]
    even = info[count + 4] == 0
    tops = (jnp.maximum(here, 0) + (TILE - 1)) // TILE
    low = jnp.minimum(later, 0) + side
    low_tile = low // TILE
    spans = ((0, tops), (low_tile, tiles))
    places = (0, bottom_tile)
    edges = (tops - 1, low_tile)

    def rows(tile):
        return pl.ds(pl.multiple_of(tile * TILE, TILE), TILE)

    def load(half, tile, source):
        return pltpu.make_async_copy(
            source.at[rows(tile)], held.at[half, rows(tile)], load_sems.at[half, tile]
        )

    def save(half, tile):
        return pltpu.make_async_copy(
            held.at[half, rows(tile)],
            out_ref.at[rows(places[half] + tile)],
            save_sems.at[half, tile],
        )

    def old(half):
        return pltpu.make_async_copy(
            out_ref.at[rows(places[half] + edges[half])], border.at[half], edge_sems.at[half]
        )

    def start_load(half):
        def run(tile, carry):
            from_outer = even if half == 0 else jnp.logical_not(even)

            @pl.when(from_outer)
            def _():
                load(half, tile, outer_ref).start()

            @pl.when(jnp.logical_not(from_outer))
            def _():
                load(half, tile, inner_ref).start()

            return carry

        return run

    def end_load(half):
        def run(tile, carry):
            load(half, tile, outer_ref).wait()
            return carry

        return run

    def start_save(half):
        def run(tile, carry):
            save(half, tile).start()
            return carry

        return run

    def end_save(half):
        def run(tile, carry):
            save(half, tile).wait()
            return carry

        return run

    for half in (0, 1):
        low_end, high_end = spans[half]

        @pl.when(low_end < high_end)
        def _():
            old(half).start()
            lax.fori_loop(low_end, high_end, start_load(half), 0)

    for half in (0, 1):
        low_end, high_end = spans[half]

        @pl.when(low_end < high_end)
        def _():
            old(half).wait()
            lax.fori_loop(low_end, high_end, end_load(half), 0)
            row = lax.broadcasted_iota(jnp.int32, border.shape[1:], 0) + edges[half] * TILE
            new = row < here if half == 0 else row >= low
            at = rows(edges[half])
            mixed = jnp.where(
                new, held[half, at, :].astype(jnp.float32), border[half].astype(jnp.float32)
            )
            held[half, at, :] = mixed.astype(held.dtype)
            lax.fori_loop(low_end, high_end, start_save(half), 0)

    for half in (0, 1):
        lax.fori_loop(*spans[half], end_save(half), 0)


def finish(info, own, inner, outer, count):
    side, row = inner.shape
    hbm = pl.BlockSpec(memory_space=pl.ANY)
    return pl.pallas_call(
        functools.partial(finish_kernel, side, count),
        out_shape=jax.ShapeDtypeStruct(own.shape, own.dtype),
        in_specs=[pl.BlockSpec(memory_space=pltpu.SMEM), hbm, hbm, hbm],
        out_specs=hbm,
        input_output_aliases={1: 0},
        scratch_shapes=[
            pltpu.VMEM((2, side, row), own.dtype),
            pltpu.VMEM((2, TILE, row), own.dtype),
            pltpu.SemaphoreType.DMA((2, side // TILE)),
            pltpu.SemaphoreType.DMA((2,)),
            pltpu.SemaphoreType.DMA((2, side // TILE)),
        ],
        compiler_params=pltpu.CompilerParams(vmem_limit_bytes=60 * 1024 * 1024),
    )(info, own, inner, outer)


def body(frames, match, weight, keep, gain):
    count, tokens, width = frames.shape
    groups = keep.shape[1]
    kept_dev = count * groups // 2
    drift = kept_dev // 2 - count
    chunk = 2 * TILE
    side = -(-drift // chunk) * chunk
    n = lax.axis_size("seq")
    info, table, head = exchange(keep, match, weight, frames, side, chunk)
    first = lax.ppermute(head, "seq", [(i + 1, i) for i in range(n - 1)])
    batch = 4 if count % 4 == 0 and count > 4 else 1
    early = count // batch - 1
    outer, own, inner, held = merge(info, table, gain, frames, groups, side, kept_dev, batch, 0, early)
    outer, own, inner = merge(
        info,
        table,
        gain,
        frames,
        groups,
        side,
        kept_dev,
        batch,
        early,
        1,
        late=(first, held, outer, own, inner),
    )
    inner = lax.ppermute(inner, "seq", [(i, i ^ 1) for i in range(n)])
    onward = [(i, i + 1) for i in range(1, n - 1, 2)]
    backward = [(j, i) for i, j in onward]

    def still(outer):
        return outer

    def forth(rows):
        def run(outer):
            moved = lax.ppermute(outer[:rows], "seq", onward)
            return jnp.pad(moved, ((0, side - rows), (0, 0)))

        return run

    def back(rows):
        def run(outer):
            moved = lax.ppermute(outer[side - rows :], "seq", backward)
            return jnp.pad(moved, ((side - rows, 0), (0, 0)))

        return run

    sizes = range(chunk, side + 1, chunk)
    branches = [still] + [forth(rows) for rows in sizes] + [back(rows) for rows in sizes]
    outer = lax.switch(info[count + 3], branches, outer)
    return finish(info, own, inner, outer, count)


def solution(mesh):
    placed = (
        P(("groups", "seq"), None, None),
        P(("groups", "seq"), None),
        P(("groups", "seq"), None),
        P(("groups", "seq"), None),
        P(),
    )
    return jax.shard_map(
        body, mesh=mesh, in_specs=placed, out_specs=P(("groups", "seq"), None), check_vma=False
    )
```

```python
import functools

import jax
import jax.numpy as jnp
from jax import lax
from jax.experimental import pallas as pl
from jax.experimental.pallas import tpu as pltpu
from jax.sharding import PartitionSpec as P

TILE = 16


def exchange_kernel(
    n,
    side,
    chunk,
    keep_ref,
    match_ref,
    weight_ref,
    frames_ref,
    info_ref,
    table_ref,
    first_ref,
    everyone,
    own,
    send_sem,
    recv_sem,
    frame_sems,
):
    count, groups = keep_ref.shape
    tokens = match_ref.shape[1]
    per = tokens // groups
    kept_dev = count * groups // 2
    me = lax.axis_index("seq")
    barrier = pltpu.get_barrier_semaphore()

    def greet(step, carry):
        peer = lax.rem(me + step, n)
        pl.semaphore_signal(
            barrier, inc=1, device_id={"seq": peer}, device_id_type=pl.DeviceIdType.MESH
        )
        return carry

    lax.fori_loop(1, n, greet, 0)
    keep = keep_ref[...].astype(jnp.float32)
    own[0:1, :] = match_ref[0:1, :]
    own[1:2, :] = weight_ref[0:1, :]
    total = jnp.sum(keep, keepdims=True).astype(jnp.int32)
    own[2:8, :] = jnp.broadcast_to(total, (6, tokens))
    everyone[pl.ds(me, 1)] = own[...][None]
    pl.semaphore_wait(barrier, n - 1)

    def copy(step):
        peer = lax.rem(me + step, n)
        return pltpu.make_async_remote_copy(
            src_ref=own,
            dst_ref=everyone.at[me],
            send_sem=send_sem.at[step],
            recv_sem=recv_sem.at[step],
            device_id={"seq": peer},
            device_id_type=pl.DeviceIdType.MESH,
        )

    def send(step, carry):
        copy(step).start()
        return carry

    def finish(step, carry):
        copy(step).wait()
        return carry

    lax.fori_loop(1, n, send, 0)
    frame_copy = pltpu.make_async_remote_copy(
        src_ref=frames_ref.at[pl.ds(0, 1)],
        dst_ref=first_ref,
        send_sem=frame_sems.at[0],
        recv_sem=frame_sems.at[1],
        device_id={"seq": lax.rem(me + n - 1, n)},
        device_id_type=pl.DeviceIdType.MESH,
    )
    @pl.when(me > 0)
    def _():
        frame_copy.start()

    frame = lax.broadcasted_iota(jnp.int32, keep.shape, 0)
    earlier = [
        jnp.sum(jnp.where(frame < f, keep, 0.0)).astype(jnp.int32) for f in range(count + 1)
    ]
    kept_bits = keep.astype(jnp.bfloat16)
    g = lax.broadcasted_iota(jnp.int32, (groups, tokens), 0)
    t_group = lax.broadcasted_iota(jnp.int32, (groups, tokens), 1) // per
    below = (g < t_group).astype(jnp.bfloat16)
    same = (g == t_group).astype(jnp.bfloat16)
    before = jnp.dot(kept_bits, below, preferred_element_type=jnp.float32)
    kept = jnp.dot(kept_bits, same, preferred_element_type=jnp.float32)
    table_ref[0] = jnp.where(kept > 0.5, before.astype(jnp.int32), -10000)
    table_ref[4] = weight_ref[...]
    at = lax.broadcasted_iota(jnp.int32, (groups, groups), 0)
    other = lax.broadcasted_iota(jnp.int32, (groups, groups), 1)
    column = lax.dot_general(
        (other < at).astype(jnp.bfloat16),
        kept_bits,
        (((1,), (1,)), ((), ())),
        preferred_element_type=jnp.float32,
    )

    def incoming(k, target, heavy):
        place = jnp.sum(
            jnp.where(g == target // per, column[:, k : k + 1], 0.0), axis=0, keepdims=True
        )
        table_ref[1, k : k + 1, :] = jnp.where(target >= 0, place.astype(jnp.int32), -10000)
        table_ref[2, k : k + 1, :] = target % per
        table_ref[3, k : k + 1, :] = heavy

    for k in range(count - 1):
        incoming(k, match_ref[k + 1 : k + 2, :], weight_ref[k + 1 : k + 2, :])
    lax.fori_loop(1, n, finish, 0)
    counts = (everyone[:, 2, :] - kept_dev).astype(jnp.float32)
    device = lax.broadcasted_iota(jnp.int32, counts.shape, 0)
    lane = lax.broadcasted_iota(jnp.int32, counts.shape, 1)
    counts = jnp.where(lane == 0, counts, 0.0)
    here = jnp.sum(jnp.where(device < me, counts, 0.0)).astype(jnp.int32)
    later = jnp.sum(jnp.where(device <= me, counts, 0.0)).astype(jnp.int32)
    for f in range(count + 1):
        info_ref[f] = earlier[f] + (here + side)
    odd = lax.rem(me, 2)
    outer = jnp.where(odd == 1, later, here)
    pieces = (jnp.abs(outer) + (chunk - 1)) // chunk
    info_ref[count + 1] = here
    info_ref[count + 2] = later
    info_ref[count + 3] = jnp.where(outer < 0, pieces + side // chunk, pieces)
    info_ref[count + 4] = odd
    info_ref[count + 5] = jnp.where(me == n - 1, 1, 0)
    block = everyone[jnp.minimum(me + 1, n - 1)]
    incoming(count - 1, block[0:1, :], jnp.where(me == n - 1, 0, block[1:2, :]))

    @pl.when(me > 0)
    def _():
        frame_copy.wait_send()

    @pl.when(me < n - 1)
    def _():
        frame_copy.wait_recv()


def exchange(keep, match, weight, frames, side, chunk):
    n = lax.axis_size("seq")
    count, tokens = match.shape
    whole = pl.BlockSpec(memory_space=pltpu.VMEM)
    return pl.pallas_call(
        functools.partial(exchange_kernel, n, side, chunk),
        out_shape=[
            jax.ShapeDtypeStruct((count + 6,), jnp.int32),
            jax.ShapeDtypeStruct((5, count, tokens), jnp.int32),
            jax.ShapeDtypeStruct((1,) + frames.shape[1:], frames.dtype),
        ],
        in_specs=[whole] * 3 + [pl.BlockSpec(memory_space=pl.ANY)],
        out_specs=[
            pl.BlockSpec(memory_space=pltpu.SMEM),
            whole,
            pl.BlockSpec(memory_space=pl.ANY),
        ],
        scratch_shapes=[
            pltpu.VMEM((n, 8, tokens), jnp.int32),
            pltpu.VMEM((8, tokens), jnp.int32),
            pltpu.SemaphoreType.DMA((n,)),
            pltpu.SemaphoreType.DMA((n,)),
            pltpu.SemaphoreType.DMA((2,)),
        ],
        compiler_params=pltpu.CompilerParams(collective_id=0, has_side_effects=True),
    )(keep, match, weight, frames)


def merge_kernel(
    side,
    info,
    table_ref,
    gain_ref,
    frame_ref,
    after_ref,
    first_ref,
    outer_ref,
    own_ref,
    inner_ref,
    window,
    sems,
):
    count = table_ref.shape[1]
    batch, tokens, width = frame_ref.shape
    per = own_ref.shape[1] // width
    groups = tokens // per
    kept_dev = own_ref.shape[0]
    edge = side // TILE
    tiles = (2 * side + kept_dev) // TILE
    f = pl.program_id(0)
    odd = info[count + 4]
    last = f == pl.num_programs(0) - 1
    lead = f * batch
    starts = [info[lead + k] for k in range(batch + 1)]
    bases = [pl.multiple_of((start // TILE) * TILE, TILE) for start in starts[:-1]]
    need = starts[1] - bases[0]
    for k in range(1, batch):
        need = jnp.maximum(need, starts[k + 1] - bases[k])

    def work(rows):
        high = per * rows
        line = lax.broadcasted_iota(jnp.int32, (high, tokens), 0)
        part = lax.broadcasted_iota(jnp.int32, (1, tokens), 1) % per * rows
        ready = []
        for k in range(batch):
            at = pl.ds(lead + k, 1)
            off = starts[k] - bases[k]
            own_key = table_ref[0, at, :] + off + part
            inc_key = table_ref[1, at, :] + off + table_ref[2, at, :] * rows
            mine = jnp.where(line == own_key, table_ref[4, at, :].astype(jnp.float32), 0.0)
            theirs = jnp.where(line == inc_key, table_ref[3, at, :].astype(jnp.float32), 0.0)
            total = jnp.maximum(jnp.sum(mine + theirs, axis=1, keepdims=True), 1.0)
            if k + 1 < batch:
                later = frame_ref[k + 1]
            else:
                end = jnp.where(info[count + 5] == 1, jnp.zeros_like(first_ref[0]), first_ref[0])
                later = jnp.where(last, end, after_ref[0])
            summed = jnp.dot(
                mine.astype(jnp.bfloat16), frame_ref[k], preferred_element_type=jnp.float32
            ) + jnp.dot(theirs.astype(jnp.bfloat16), later, preferred_element_type=jnp.float32)
            mean = jnp.sum(summed * summed, axis=1, keepdims=True) * (1.0 / width)
            scale = lax.rsqrt(mean + 1e-06 * total * total)
            ready.append(summed * scale * gain_ref[...][None, :])
        for k in range(batch):
            base = bases[k]
            normed = ready[k]
            old_rows = lax.broadcasted_iota(jnp.int32, (TILE, width), 0) < starts[k] - base
            for j in range(per):
                cols = slice(j * width, (j + 1) * width)
                old = window[pl.ds(base, TILE), cols].astype(jnp.float32)
                head = jnp.where(old_rows, old, normed[j * rows : j * rows + TILE])
                window[pl.ds(base, TILE), cols] = head.astype(jnp.bfloat16)
                window[pl.ds(pl.multiple_of(base + TILE, TILE), rows - TILE), cols] = normed[
                    j * rows + TILE : (j + 1) * rows
                ].astype(jnp.bfloat16)

    @pl.when(need <= 48)
    def _():
        work(48)

    @pl.when((need > 48) & (need <= 64))
    def _():
        work(64)

    @pl.when(need > 64)
    def _():
        work(groups + TILE)

    def send(tile, target, place):
        pltpu.make_async_copy(
            window.at[pl.ds(pl.multiple_of(tile * TILE, TILE), TILE)],
            target.at[pl.ds(pl.multiple_of(place * TILE, TILE), TILE)],
            sems.at[tile],
        ).start()

    def flush(tile, carry):
        top = tile < edge
        end = tile >= tiles - edge

        @pl.when(top & (odd == 0))
        def _():
            send(tile, outer_ref, tile)

        @pl.when(top & (odd == 1))
        def _():
            send(tile, inner_ref, tile)

        @pl.when(jnp.logical_not(top | end))
        def _():
            send(tile, own_ref, tile - edge)

        @pl.when(end & (odd == 0))
        def _():
            send(tile, inner_ref, tile - (tiles - edge))

        @pl.when(end & (odd == 1))
        def _():
            send(tile, outer_ref, tile - (tiles - edge))

        return carry

    lax.fori_loop(
        jnp.where(f == 0, 0, starts[0] // TILE),
        jnp.where(last, tiles, starts[batch] // TILE),
        flush,
        0,
    )

    @pl.when(last)
    def _():
        for tile in range(tiles):
            pltpu.make_async_copy(
                window.at[pl.ds(tile * TILE, TILE)], own_ref.at[pl.ds(0, TILE)], sems.at[tile]
            ).wait()


def merge(info, table, gain, frames, first, groups, side, kept_dev):
    count, tokens, width = frames.shape
    batch = 4 if count % 4 == 0 else 1
    row = tokens // groups * width
    whole = pl.BlockSpec(memory_space=pltpu.VMEM)
    return pl.pallas_call(
        functools.partial(merge_kernel, side),
        out_shape=[
            jax.ShapeDtypeStruct((side, row), jnp.bfloat16),
            jax.ShapeDtypeStruct((kept_dev, row), jnp.bfloat16),
            jax.ShapeDtypeStruct((side, row), jnp.bfloat16),
        ],
        grid_spec=pltpu.PrefetchScalarGridSpec(
            num_scalar_prefetch=1,
            grid=(count // batch,),
            in_specs=[
                whole,
                whole,
                pl.BlockSpec((batch, tokens, width), lambda f, s: (f, 0, 0)),
                pl.BlockSpec(
                    (1, tokens, width), lambda f, s: (jnp.minimum((f + 1) * batch, count - 1), 0, 0)
                ),
                pl.BlockSpec((1, tokens, width), lambda f, s: (0, 0, 0)),
            ],
            out_specs=[pl.BlockSpec(memory_space=pl.ANY)] * 3,
            scratch_shapes=[
                pltpu.VMEM((2 * side + kept_dev + groups + TILE, row), jnp.bfloat16),
                pltpu.SemaphoreType.DMA(((2 * side + kept_dev) // TILE,)),
            ],
        ),
        compiler_params=pltpu.CompilerParams(vmem_limit_bytes=60 * 1024 * 1024),
    )(info, table, gain, frames, frames, first)


def finish_kernel(
    side, count, info, own_ref, inner_ref, outer_ref, out_ref, held, border, load_sems, edge_sems, save_sems
):
    tiles = side // TILE
    bottom_tile = (out_ref.shape[0] - side) // TILE
    here = info[count + 1]
    later = info[count + 2]
    even = info[count + 4] == 0
    tops = (jnp.maximum(here, 0) + (TILE - 1)) // TILE
    low = jnp.minimum(later, 0) + side
    low_tile = low // TILE
    spans = ((0, tops), (low_tile, tiles))
    places = (0, bottom_tile)
    edges = (tops - 1, low_tile)

    def rows(tile):
        return pl.ds(pl.multiple_of(tile * TILE, TILE), TILE)

    def load(half, tile, source):
        return pltpu.make_async_copy(
            source.at[rows(tile)], held.at[half, rows(tile)], load_sems.at[half, tile]
        )

    def save(half, tile):
        return pltpu.make_async_copy(
            held.at[half, rows(tile)],
            out_ref.at[rows(places[half] + tile)],
            save_sems.at[half, tile],
        )

    def straight(half, tile):
        return pltpu.make_async_copy(
            outer_ref.at[rows(tile)],
            out_ref.at[rows(places[half] + tile)],
            save_sems.at[half, tile],
        )

    def old(half):
        return pltpu.make_async_copy(
            out_ref.at[rows(places[half] + edges[half])], border.at[half], edge_sems.at[half]
        )

    def staged(half, tile):
        from_outer = even if half == 0 else jnp.logical_not(even)
        return jnp.logical_not(from_outer) | (tile == edges[half])

    def start_load(half):
        def run(tile, carry):
            from_outer = even if half == 0 else jnp.logical_not(even)

            @pl.when(from_outer & (tile == edges[half]))
            def _():
                load(half, tile, outer_ref).start()

            @pl.when(from_outer & (tile != edges[half]))
            def _():
                straight(half, tile).start()

            @pl.when(jnp.logical_not(from_outer))
            def _():
                load(half, tile, inner_ref).start()

            return carry

        return run

    def end_load(half):
        def run(tile, carry):
            @pl.when(staged(half, tile))
            def _():
                load(half, tile, outer_ref).wait()

            return carry

        return run

    def start_save(half):
        def run(tile, carry):
            @pl.when(staged(half, tile))
            def _():
                save(half, tile).start()

            return carry

        return run

    def end_save(half):
        def run(tile, carry):
            save(half, tile).wait()
            return carry

        return run

    for half in (0, 1):
        low_end, high_end = spans[half]

        @pl.when(low_end < high_end)
        def _():
            old(half).start()
            lax.fori_loop(low_end, high_end, start_load(half), 0)

    for half in (0, 1):
        low_end, high_end = spans[half]

        @pl.when(low_end < high_end)
        def _():
            old(half).wait()
            lax.fori_loop(low_end, high_end, end_load(half), 0)
            row = lax.broadcasted_iota(jnp.int32, border.shape[1:], 0) + edges[half] * TILE
            new = row < here if half == 0 else row >= low
            at = rows(edges[half])
            mixed = jnp.where(
                new, held[half, at, :].astype(jnp.float32), border[half].astype(jnp.float32)
            )
            held[half, at, :] = mixed.astype(held.dtype)
            lax.fori_loop(low_end, high_end, start_save(half), 0)

    for half in (0, 1):
        lax.fori_loop(*spans[half], end_save(half), 0)


def finish(info, own, inner, outer, count):
    side, row = inner.shape
    hbm = pl.BlockSpec(memory_space=pl.ANY)
    return pl.pallas_call(
        functools.partial(finish_kernel, side, count),
        out_shape=jax.ShapeDtypeStruct(own.shape, own.dtype),
        in_specs=[pl.BlockSpec(memory_space=pltpu.SMEM), hbm, hbm, hbm],
        out_specs=hbm,
        input_output_aliases={1: 0},
        scratch_shapes=[
            pltpu.VMEM((2, side, row), own.dtype),
            pltpu.VMEM((2, TILE, row), own.dtype),
            pltpu.SemaphoreType.DMA((2, side // TILE)),
            pltpu.SemaphoreType.DMA((2,)),
            pltpu.SemaphoreType.DMA((2, side // TILE)),
        ],
        compiler_params=pltpu.CompilerParams(vmem_limit_bytes=60 * 1024 * 1024),
    )(info, own, inner, outer)


def body(frames, match, weight, keep, gain):
    count, tokens, width = frames.shape
    groups = keep.shape[1]
    kept_dev = count * groups // 2
    drift = kept_dev // 2 - count
    chunk = TILE
    side = -(-drift // chunk) * chunk
    n = lax.axis_size("seq")
    info, table, first = exchange(keep, match, weight, frames, side, chunk)
    outer, own, inner = merge(
        info, table, gain, frames, first, groups, side, kept_dev
    )
    inner = lax.ppermute(inner, "seq", [(i, i ^ 1) for i in range(n)])
    onward = [(i, i + 1) for i in range(1, n - 1, 2)]
    backward = [(j, i) for i, j in onward]

    def still(outer):
        return outer

    def forth(rows):
        def run(outer):
            moved = lax.ppermute(outer[:rows], "seq", onward)
            return jnp.pad(moved, ((0, side - rows), (0, 0)))

        return run

    def back(rows):
        def run(outer):
            moved = lax.ppermute(outer[side - rows :], "seq", backward)
            return jnp.pad(moved, ((side - rows, 0), (0, 0)))

        return run

    sizes = range(chunk, side + 1, chunk)
    branches = [still] + [forth(rows) for rows in sizes] + [back(rows) for rows in sizes]
    outer = lax.switch(info[count + 3], branches, outer)
    return finish(info, own, inner, outer, count)


def solution(mesh):
    placed = (
        P(("groups", "seq"), None, None),
        P(("groups", "seq"), None),
        P(("groups", "seq"), None),
        P(("groups", "seq"), None),
        P(),
    )
    return jax.shard_map(
        body, mesh=mesh, in_specs=placed, out_specs=P(("groups", "seq"), None), check_vma=False
    )
```

```python
import functools

import jax
import jax.numpy as jnp
from jax import lax
from jax.experimental import pallas as pl
from jax.experimental.pallas import tpu as pltpu
from jax.sharding import PartitionSpec as P

TILE = 16


def exchange_kernel(
    n,
    side,
    chunk,
    keep_ref,
    match_ref,
    weight_ref,
    frames_ref,
    info_ref,
    table_ref,
    first_ref,
    everyone,
    own,
    send_sem,
    recv_sem,
    frame_sems,
):
    count, groups = keep_ref.shape
    tokens = match_ref.shape[1]
    per = tokens // groups
    kept_dev = count * groups // 2
    me = lax.axis_index("seq")
    barrier = pltpu.get_barrier_semaphore()

    def greet(step, carry):
        peer = lax.rem(me + step, n)
        pl.semaphore_signal(
            barrier, inc=1, device_id={"seq": peer}, device_id_type=pl.DeviceIdType.MESH
        )
        return carry

    lax.fori_loop(1, n, greet, 0)
    keep = keep_ref[...].astype(jnp.float32)
    own[0:1, :] = match_ref[0:1, :]
    own[1:2, :] = weight_ref[0:1, :]
    total = jnp.sum(keep, keepdims=True).astype(jnp.int32)
    own[2:8, :] = jnp.broadcast_to(total, (6, tokens))
    everyone[pl.ds(me, 1)] = own[...][None]
    pl.semaphore_wait(barrier, n - 1)

    def copy(step):
        peer = lax.rem(me + step, n)
        return pltpu.make_async_remote_copy(
            src_ref=own,
            dst_ref=everyone.at[me],
            send_sem=send_sem.at[step],
            recv_sem=recv_sem.at[step],
            device_id={"seq": peer},
            device_id_type=pl.DeviceIdType.MESH,
        )

    def send(step, carry):
        copy(step).start()
        return carry

    def finish(step, carry):
        copy(step).wait()
        return carry

    frame_copy = pltpu.make_async_remote_copy(
        src_ref=frames_ref.at[pl.ds(0, 1)],
        dst_ref=first_ref,
        send_sem=frame_sems.at[0],
        recv_sem=frame_sems.at[1],
        device_id={"seq": lax.rem(me + n - 1, n)},
        device_id_type=pl.DeviceIdType.MESH,
    )
    @pl.when(me > 0)
    def _():
        frame_copy.start()

    lax.fori_loop(1, n, send, 0)
    frame = lax.broadcasted_iota(jnp.int32, keep.shape, 0)
    earlier = [
        jnp.sum(jnp.where(frame < f, keep, 0.0)).astype(jnp.int32) for f in range(count + 1)
    ]
    kept_bits = keep.astype(jnp.bfloat16)
    g = lax.broadcasted_iota(jnp.int32, (groups, tokens), 0)
    t_group = lax.broadcasted_iota(jnp.int32, (groups, tokens), 1) // per
    below = (g < t_group).astype(jnp.bfloat16)
    same = (g == t_group).astype(jnp.bfloat16)
    before = jnp.dot(kept_bits, below, preferred_element_type=jnp.float32)
    kept = jnp.dot(kept_bits, same, preferred_element_type=jnp.float32)
    table_ref[0] = jnp.where(kept > 0.5, before.astype(jnp.int32), -10000)
    table_ref[4] = weight_ref[...]
    at = lax.broadcasted_iota(jnp.int32, (groups, groups), 0)
    other = lax.broadcasted_iota(jnp.int32, (groups, groups), 1)
    column = lax.dot_general(
        (other < at).astype(jnp.bfloat16),
        kept_bits,
        (((1,), (1,)), ((), ())),
        preferred_element_type=jnp.float32,
    )

    def incoming(k, target, heavy):
        place = jnp.sum(
            jnp.where(g == target // per, column[:, k : k + 1], 0.0), axis=0, keepdims=True
        )
        table_ref[1, k : k + 1, :] = jnp.where(target >= 0, place.astype(jnp.int32), -10000)
        table_ref[2, k : k + 1, :] = target % per
        table_ref[3, k : k + 1, :] = heavy

    for k in range(count - 1):
        incoming(k, match_ref[k + 1 : k + 2, :], weight_ref[k + 1 : k + 2, :])
    lax.fori_loop(1, n, finish, 0)
    counts = (everyone[:, 2, :] - kept_dev).astype(jnp.float32)
    device = lax.broadcasted_iota(jnp.int32, counts.shape, 0)
    lane = lax.broadcasted_iota(jnp.int32, counts.shape, 1)
    counts = jnp.where(lane == 0, counts, 0.0)
    here = jnp.sum(jnp.where(device < me, counts, 0.0)).astype(jnp.int32)
    later = jnp.sum(jnp.where(device <= me, counts, 0.0)).astype(jnp.int32)
    for f in range(count + 1):
        info_ref[f] = earlier[f] + (here + side)
    odd = lax.rem(me, 2)
    outer = jnp.where(odd == 1, later, here)
    pieces = (jnp.abs(outer) + (chunk - 1)) // chunk
    info_ref[count + 1] = here
    info_ref[count + 2] = later
    info_ref[count + 3] = jnp.where(outer < 0, pieces + side // chunk, pieces)
    info_ref[count + 4] = odd
    info_ref[count + 5] = jnp.where(me == n - 1, 1, 0)
    block = everyone[jnp.minimum(me + 1, n - 1)]
    incoming(count - 1, block[0:1, :], jnp.where(me == n - 1, 0, block[1:2, :]))

    @pl.when(me > 0)
    def _():
        frame_copy.wait_send()

    @pl.when(me < n - 1)
    def _():
        frame_copy.wait_recv()


def exchange(keep, match, weight, frames, side, chunk):
    n = lax.axis_size("seq")
    count, tokens = match.shape
    whole = pl.BlockSpec(memory_space=pltpu.VMEM)
    return pl.pallas_call(
        functools.partial(exchange_kernel, n, side, chunk),
        out_shape=[
            jax.ShapeDtypeStruct((count + 6,), jnp.int32),
            jax.ShapeDtypeStruct((5, count, tokens), jnp.int32),
            jax.ShapeDtypeStruct((1,) + frames.shape[1:], frames.dtype),
        ],
        in_specs=[whole] * 3 + [pl.BlockSpec(memory_space=pl.ANY)],
        out_specs=[
            pl.BlockSpec(memory_space=pltpu.SMEM),
            whole,
            pl.BlockSpec(memory_space=pl.ANY),
        ],
        scratch_shapes=[
            pltpu.VMEM((n, 8, tokens), jnp.int32),
            pltpu.VMEM((8, tokens), jnp.int32),
            pltpu.SemaphoreType.DMA((n,)),
            pltpu.SemaphoreType.DMA((n,)),
            pltpu.SemaphoreType.DMA((2,)),
        ],
        compiler_params=pltpu.CompilerParams(collective_id=0, has_side_effects=True),
    )(keep, match, weight, frames)


def merge_kernel(
    side,
    info,
    table_ref,
    gain_ref,
    frame_ref,
    after_ref,
    first_ref,
    outer_ref,
    own_ref,
    inner_ref,
    window,
    sems,
):
    count = table_ref.shape[1]
    batch, tokens, width = frame_ref.shape
    per = own_ref.shape[1] // width
    groups = tokens // per
    kept_dev = own_ref.shape[0]
    edge = side // TILE
    tiles = (2 * side + kept_dev) // TILE
    f = pl.program_id(0)
    odd = info[count + 4]
    last = f == pl.num_programs(0) - 1
    lead = f * batch
    starts = [info[lead + k] for k in range(batch + 1)]
    bases = [pl.multiple_of((start // TILE) * TILE, TILE) for start in starts[:-1]]
    need = starts[1] - bases[0]
    for k in range(1, batch):
        need = jnp.maximum(need, starts[k + 1] - bases[k])

    def work(rows):
        high = per * rows
        line = lax.broadcasted_iota(jnp.int32, (high, tokens), 0)
        part = lax.broadcasted_iota(jnp.int32, (1, tokens), 1) % per * rows
        ready = []
        for k in range(batch):
            at = pl.ds(lead + k, 1)
            off = starts[k] - bases[k]
            own_key = table_ref[0, at, :] + off + part
            inc_key = table_ref[1, at, :] + off + table_ref[2, at, :] * rows
            mine = jnp.where(line == own_key, table_ref[4, at, :].astype(jnp.float32), 0.0)
            theirs = jnp.where(line == inc_key, table_ref[3, at, :].astype(jnp.float32), 0.0)
            total = jnp.maximum(jnp.sum(mine + theirs, axis=1, keepdims=True), 1.0)
            if k + 1 < batch:
                later = frame_ref[k + 1]
            else:
                end = jnp.where(info[count + 5] == 1, jnp.zeros_like(first_ref[0]), first_ref[0])
                later = jnp.where(last, end, after_ref[0])
            summed = jnp.dot(
                mine.astype(jnp.bfloat16), frame_ref[k], preferred_element_type=jnp.float32
            ) + jnp.dot(theirs.astype(jnp.bfloat16), later, preferred_element_type=jnp.float32)
            mean = jnp.sum(summed * summed, axis=1, keepdims=True) * (1.0 / width)
            scale = lax.rsqrt(mean + 1e-06 * total * total)
            ready.append(summed * scale * gain_ref[...][None, :])
        for k in range(batch):
            base = bases[k]
            normed = ready[k]
            old_rows = lax.broadcasted_iota(jnp.int32, (TILE, width), 0) < starts[k] - base
            for j in range(per):
                cols = slice(j * width, (j + 1) * width)
                old = window[pl.ds(base, TILE), cols].astype(jnp.float32)
                head = jnp.where(old_rows, old, normed[j * rows : j * rows + TILE])
                window[pl.ds(base, TILE), cols] = head.astype(jnp.bfloat16)
                window[pl.ds(pl.multiple_of(base + TILE, TILE), rows - TILE), cols] = normed[
                    j * rows + TILE : (j + 1) * rows
                ].astype(jnp.bfloat16)

    @pl.when(need <= 48)
    def _():
        work(48)

    @pl.when((need > 48) & (need <= 64))
    def _():
        work(64)

    @pl.when(need > 64)
    def _():
        work(groups + TILE)

    def send(tile, target, place):
        pltpu.make_async_copy(
            window.at[pl.ds(pl.multiple_of(tile * TILE, TILE), TILE)],
            target.at[pl.ds(pl.multiple_of(place * TILE, TILE), TILE)],
            sems.at[tile],
        ).start()

    def flush(tile, carry):
        top = tile < edge
        end = tile >= tiles - edge

        @pl.when(top & (odd == 0))
        def _():
            send(tile, outer_ref, tile)

        @pl.when(top & (odd == 1))
        def _():
            send(tile, inner_ref, tile)

        @pl.when(jnp.logical_not(top | end))
        def _():
            send(tile, own_ref, tile - edge)

        @pl.when(end & (odd == 0))
        def _():
            send(tile, inner_ref, tile - (tiles - edge))

        @pl.when(end & (odd == 1))
        def _():
            send(tile, outer_ref, tile - (tiles - edge))

        return carry

    lax.fori_loop(
        jnp.where(f == 0, 0, starts[0] // TILE),
        jnp.where(last, tiles, starts[batch] // TILE),
        flush,
        0,
    )

    @pl.when(last)
    def _():
        for tile in range(tiles):
            pltpu.make_async_copy(
                window.at[pl.ds(tile * TILE, TILE)], own_ref.at[pl.ds(0, TILE)], sems.at[tile]
            ).wait()


def merge(info, table, gain, frames, first, groups, side, kept_dev):
    count, tokens, width = frames.shape
    batch = 4 if count % 4 == 0 else 1
    row = tokens // groups * width
    whole = pl.BlockSpec(memory_space=pltpu.VMEM)
    return pl.pallas_call(
        functools.partial(merge_kernel, side),
        out_shape=[
            jax.ShapeDtypeStruct((side, row), jnp.bfloat16),
            jax.ShapeDtypeStruct((kept_dev, row), jnp.bfloat16),
            jax.ShapeDtypeStruct((side, row), jnp.bfloat16),
        ],
        grid_spec=pltpu.PrefetchScalarGridSpec(
            num_scalar_prefetch=1,
            grid=(count // batch,),
            in_specs=[
                whole,
                whole,
                pl.BlockSpec((batch, tokens, width), lambda f, s: (f, 0, 0)),
                pl.BlockSpec(
                    (1, tokens, width), lambda f, s: (jnp.minimum((f + 1) * batch, count - 1), 0, 0)
                ),
                pl.BlockSpec((1, tokens, width), lambda f, s: (0, 0, 0)),
            ],
            out_specs=[pl.BlockSpec(memory_space=pl.ANY)] * 3,
            scratch_shapes=[
                pltpu.VMEM((2 * side + kept_dev + groups + TILE, row), jnp.bfloat16),
                pltpu.SemaphoreType.DMA(((2 * side + kept_dev) // TILE,)),
            ],
        ),
        compiler_params=pltpu.CompilerParams(vmem_limit_bytes=60 * 1024 * 1024),
    )(info, table, gain, frames, frames, first)


def finish_kernel(
    side, count, info, own_ref, inner_ref, outer_ref, out_ref, held, border, load_sems, edge_sems, save_sems
):
    tiles = side // TILE
    bottom_tile = (out_ref.shape[0] - side) // TILE
    here = info[count + 1]
    later = info[count + 2]
    even = info[count + 4] == 0
    tops = (jnp.maximum(here, 0) + (TILE - 1)) // TILE
    low = jnp.minimum(later, 0) + side
    low_tile = low // TILE
    spans = ((0, tops), (low_tile, tiles))
    places = (0, bottom_tile)
    edges = (tops - 1, low_tile)

    def rows(tile):
        return pl.ds(pl.multiple_of(tile * TILE, TILE), TILE)

    def load(half, tile, source):
        return pltpu.make_async_copy(
            source.at[rows(tile)], held.at[half, rows(tile)], load_sems.at[half, tile]
        )

    def save(half, tile):
        return pltpu.make_async_copy(
            held.at[half, rows(tile)],
            out_ref.at[rows(places[half] + tile)],
            save_sems.at[half, tile],
        )

    def straight(half, tile):
        return pltpu.make_async_copy(
            outer_ref.at[rows(tile)],
            out_ref.at[rows(places[half] + tile)],
            save_sems.at[half, tile],
        )

    def old(half):
        return pltpu.make_async_copy(
            out_ref.at[rows(places[half] + edges[half])], border.at[half], edge_sems.at[half]
        )

    def staged(half, tile):
        from_outer = even if half == 0 else jnp.logical_not(even)
        return jnp.logical_not(from_outer) | (tile == edges[half])

    def start_load(half):
        def run(tile, carry):
            from_outer = even if half == 0 else jnp.logical_not(even)

            @pl.when(from_outer & (tile == edges[half]))
            def _():
                load(half, tile, outer_ref).start()

            @pl.when(from_outer & (tile != edges[half]))
            def _():
                straight(half, tile).start()

            @pl.when(jnp.logical_not(from_outer))
            def _():
                load(half, tile, inner_ref).start()

            return carry

        return run

    def end_load(half):
        def run(tile, carry):
            @pl.when(staged(half, tile))
            def _():
                load(half, tile, outer_ref).wait()

            return carry

        return run

    def start_save(half):
        def run(tile, carry):
            @pl.when(staged(half, tile))
            def _():
                save(half, tile).start()

            return carry

        return run

    def end_save(half):
        def run(tile, carry):
            save(half, tile).wait()
            return carry

        return run

    for half in (0, 1):
        low_end, high_end = spans[half]

        @pl.when(low_end < high_end)
        def _():
            old(half).start()
            lax.fori_loop(low_end, high_end, start_load(half), 0)

    for half in (0, 1):
        low_end, high_end = spans[half]

        @pl.when(low_end < high_end)
        def _():
            old(half).wait()
            lax.fori_loop(low_end, high_end, end_load(half), 0)
            row = lax.broadcasted_iota(jnp.int32, border.shape[1:], 0) + edges[half] * TILE
            new = row < here if half == 0 else row >= low
            at = rows(edges[half])
            mixed = jnp.where(
                new, held[half, at, :].astype(jnp.float32), border[half].astype(jnp.float32)
            )
            held[half, at, :] = mixed.astype(held.dtype)
            lax.fori_loop(low_end, high_end, start_save(half), 0)

    for half in (0, 1):
        lax.fori_loop(*spans[half], end_save(half), 0)


def finish(info, own, inner, outer, count):
    side, row = inner.shape
    hbm = pl.BlockSpec(memory_space=pl.ANY)
    return pl.pallas_call(
        functools.partial(finish_kernel, side, count),
        out_shape=jax.ShapeDtypeStruct(own.shape, own.dtype),
        in_specs=[pl.BlockSpec(memory_space=pltpu.SMEM), hbm, hbm, hbm],
        out_specs=hbm,
        input_output_aliases={1: 0},
        scratch_shapes=[
            pltpu.VMEM((2, side, row), own.dtype),
            pltpu.VMEM((2, TILE, row), own.dtype),
            pltpu.SemaphoreType.DMA((2, side // TILE)),
            pltpu.SemaphoreType.DMA((2,)),
            pltpu.SemaphoreType.DMA((2, side // TILE)),
        ],
        compiler_params=pltpu.CompilerParams(vmem_limit_bytes=60 * 1024 * 1024),
    )(info, own, inner, outer)


def body(frames, match, weight, keep, gain):
    count, tokens, width = frames.shape
    groups = keep.shape[1]
    kept_dev = count * groups // 2
    drift = kept_dev // 2 - count
    chunk = TILE
    side = -(-drift // chunk) * chunk
    n = lax.axis_size("seq")
    info, table, first = exchange(keep, match, weight, frames, side, chunk)
    outer, own, inner = merge(
        info, table, gain, frames, first, groups, side, kept_dev
    )
    inner = lax.ppermute(inner, "seq", [(i, i ^ 1) for i in range(n)])
    onward = [(i, i + 1) for i in range(1, n - 1, 2)]
    backward = [(j, i) for i, j in onward]

    def still(outer):
        return outer

    def forth(rows):
        def run(outer):
            moved = lax.ppermute(outer[:rows], "seq", onward)
            return jnp.pad(moved, ((0, side - rows), (0, 0)))

        return run

    def back(rows):
        def run(outer):
            moved = lax.ppermute(outer[side - rows :], "seq", backward)
            return jnp.pad(moved, ((side - rows, 0), (0, 0)))

        return run

    sizes = range(chunk, side + 1, chunk)
    branches = [still] + [forth(rows) for rows in sizes] + [back(rows) for rows in sizes]
    outer = lax.switch(info[count + 3], branches, outer)
    return finish(info, own, inner, outer, count)


def solution(mesh):
    placed = (
        P(("groups", "seq"), None, None),
        P(("groups", "seq"), None),
        P(("groups", "seq"), None),
        P(("groups", "seq"), None),
        P(),
    )
    return jax.shard_map(
        body, mesh=mesh, in_specs=placed, out_specs=P(("groups", "seq"), None), check_vma=False
    )
```
